32 devices in a mesh: section: 4 (over y, core), dp: 8 (over z, x).
Axes of the slice: x: 2, y: 2, z: 4, core: 2. Of those that a mesh axis runs over, the one named last changes fastest.
Arguments:
- activations: bfloat16 [2, 8, 1152, 512], P(None, 'dp', 'section'), may hold values from -6 to 6
- cotangent: bfloat16 [2, 8, 1152, 512], P(None, 'dp', 'section'), may hold values from -6 to 6
- article_ids: int32 [2, 8, 1152], P(None, 'dp'), may hold values from 0 to 2, as said below
- section_proj: bfloat16 [4, 512, 1536], P('section'), may hold values from -0.25 to 0.25
- out_rows: bfloat16 [1024, 512], P('section'), may hold values from -1.5 to 1.5
- up_rows: bfloat16 [1024, 2048], P('section'), may hold values from -0.25 to 0.25
- down_rows: bfloat16 [4096, 512], P('section'), may hold values from -0.125 to 0.125
- norm_gains: bfloat16 [4, 512], P('section'), may hold values from 0.5 to 1.5
- slopes: bfloat16 [4, 4], P('section'), may hold values from 0.0029907227 to 0.099609375
Outputs:
- results: bfloat16 [2, 8, 1152, 512], P(None, 'dp', 'section')
- input_grad: float32 [2, 8, 1152, 512], P(None, 'dp', 'section')
- grad_section_proj: float32 [4, 512, 1536], P('section')
- grad_out_rows: float32 [1024, 512], P('section')
- grad_up_rows: float32 [1024, 2048], P('section')
- grad_down_rows: float32 [4096, 512], P('section')
- grad_norm_gains: float32 [4, 512], P('section')
- grad_slopes: float32 [4, 4], P('section')
The draws below stay inside these ranges and needn't reach their ends.
Inputs may be any that keep to these rules, and one draw needn't show every extreme that they name: `article_ids`: along each row the ids never fall and every row holds the three articles 0, 1 and 2; in every row one of them holds bytes of both the first and the last quarter of the row.
All inputs are finite; a program needn't handle non-finite values.
Results may differ from the reference program's by a relative error of at most 0.025.
Values may be sent and summed in bfloat16 or wider, within the bound.
A program may use at most 448 MiB of HBM per device.

```python
import math
import jax
import jax.numpy as jnp
from jax import lax

D = 512
HEADS = 8
FF = 2048
SECTIONS = 4
M = 2
L = 1152
ROWS = 8


def draw_article_ids(key, part):
    key = jax.random.fold_in(key, 7)
    pattern_key, early_key, spread_key, middle_key = jax.random.split(key, 4)
    quarter_len = L // 4
    row_grid = (M, ROWS)
    pattern = jax.random.randint(pattern_key, row_grid, 0, 3)
    early = jax.random.randint(early_key, row_grid, 0, quarter_len // 2)
    spread = jax.random.randint(spread_key, row_grid, 0, quarter_len // 2 - 1)
    middle = jax.random.randint(middle_key, row_grid, 0, quarter_len - 1)
    first_bound = jnp.where(pattern == 0, 3 * quarter_len + 1 + early, jnp.where(pattern == 1, 1 + middle, 1 + early))
    second_bound = jnp.where(pattern == 1, 3 * quarter_len + 1 + early, first_bound + 1 + spread)
    positions = jnp.arange(L, dtype=jnp.int32)
    after_first = (positions[None, None, :] >= first_bound[..., None]).astype(jnp.int32)
    after_second = (positions[None, None, :] >= second_bound[..., None]).astype(jnp.int32)
    return after_first + after_second


def block_levels(rng, shape, cuts, least, top_value):
    def one(dim, shards_of):
        heights = jax.random.uniform(jax.random.fold_in(jax.random.fold_in(rng, 6), dim), (shards_of,), jnp.float32, least / len(cuts), top_value / len(cuts))
        return jnp.repeat(jnp.exp(heights), shape[dim] // shards_of).reshape((-1,) + (1,) * (len(shape) - dim - 1))

    factor_of = one(*cuts[0])
    for cut in cuts[1:]:
        factor_of = factor_of * one(*cut)
    return factor_of


def bell_draw(key, shape, scale, bound, cuts=(), kind=jnp.bfloat16):
    drawn = scale * jax.random.normal(key, shape, jnp.float32)
    if cuts:
        drawn = drawn * block_levels(key, shape, cuts, -0.22, 0.18)
    return jnp.clip(drawn, -bound, bound).astype(kind)


def setup_inputs(seed: int = 0) -> dict:
    key_of = jax.random.split(jax.random.key(seed), 10)
    return {
        "activations": bell_draw(key_of[0], (M, ROWS, L, D), 1.0, 6.0, ((1, 8), (2, 4))),
        "cotangent": bell_draw(key_of[1], (M, ROWS, L, D), 1.0, 6.0, ((1, 8), (2, 4))),
        "article_ids": draw_article_ids(jax.random.fold_in(key_of[9], 71), 0),
        "section_proj": bell_draw(key_of[3], (SECTIONS, D, 3 * D), D ** -0.5, 0.25, ((0, 4),)),
        "out_rows": bell_draw(key_of[4], (2 * D, D), (D // 32) ** -0.5, 1.5, ((0, 4),)),
        "up_rows": bell_draw(key_of[5], (2 * D, FF), D ** -0.5, 0.25, ((0, 4),)),
        "down_rows": bell_draw(key_of[6], (2 * FF, D), FF ** -0.5, 0.125, ((0, 4),)),
        "norm_gains": jnp.clip(1.0 + 0.1 * jax.random.normal(key_of[7], (SECTIONS, D), jnp.float32), 0.5, 1.5).astype(jnp.bfloat16),
        "slopes": jnp.clip(jnp.exp(math.log(0.099609375) - 3.5057412 * jax.random.uniform(key_of[8], (SECTIONS, HEADS // 2), jnp.float32) ** block_levels(key_of[8], (SECTIONS, HEADS // 2), ((0, 4),), -0.2, 0.2)), 0.0029907227, 0.099609375).astype(jnp.bfloat16),
    }


@jax.custom_vjp
def low(v):
    return lax.optimization_barrier(v.astype(jnp.bfloat16)).astype(jnp.float32)

@jax.custom_vjp
def low_back(v):
    return v

def low_keep(v):
    return (low(v), None)

def low_pass(kept, grad):
    return (grad,)

def back_keep(v):
    return (v, None)

def back_low(kept, grad):
    return (low(grad),)
low.defvjp(low_keep, low_pass)
low_back.defvjp(back_keep, back_low)
EPSILON = 1e-05
MASKED = -1e+30

def product(left, right):
    return jnp.dot(left, right, precision=lax.Precision.HIGHEST, preferred_element_type=jnp.float32)

def layer_norm(value):
    centred = value - lax.optimization_barrier(jnp.mean(value, axis=-1, keepdims=True))
    return centred * lax.rsqrt(lax.optimization_barrier(jnp.mean(centred * centred, axis=-1, keepdims=True)) + EPSILON)

def residual_block(hidden_state, id_row, weight_group):
    query_key_value_weight, out_weight, expansion_weight, down_weight, paired_gains, slope_heads = weight_group
    length, width = hidden_state.shape
    head_count = slope_heads.shape[0]
    head_dim = width // head_count
    normalized_rows = low(layer_norm(hidden_state) * paired_gains[0])
    mixed = product(normalized_rows, query_key_value_weight)
    queries = low_back(low(mixed[:, :width])).reshape(length, head_count, head_dim)
    key_rows = low_back(low(mixed[:, width:2 * width])).reshape(length, head_count, head_dim)
    value_rows = low_back(low(mixed[:, 2 * width:])).reshape(length, head_count, head_dim)
    scores = jnp.einsum('qhd,khd->hqk', queries, key_rows, precision=lax.Precision.HIGHEST, preferred_element_type=jnp.float32) * head_dim ** (-0.5)
    positions = jnp.arange(length)
    distance = (positions[:, None] - positions[None, :]).astype(jnp.float32)
    scores = low_back(scores - slope_heads[:, None, None] * distance)
    allowed = (distance >= 0) & (id_row[:, None] == id_row[None, :])
    weights_soft = jax.nn.softmax(jnp.where(allowed[None], scores, MASKED), axis=-1)
    attended = jnp.einsum('hqk,khd->qhd', low(weights_soft), value_rows, precision=lax.Precision.HIGHEST, preferred_element_type=jnp.float32).reshape(length, width)
    attended = low_back(low(attended))
    middle_state = hidden_state + low_back(product(attended, out_weight))
    second_normalized = low(layer_norm(middle_state) * paired_gains[1])
    up_raw = low_back(product(second_normalized, expansion_weight))
    activ = low(jax.nn.gelu(up_raw))
    return middle_state + low_back(product(activ, down_weight))

def one_row(weight_set, acts_row, id_row):
    first_block, second_block, pool_weight, expansion_weight = weight_set
    length, width = acts_row.shape
    h_one = low_back(low(residual_block(acts_row, id_row, first_block)))
    earlier = jnp.concatenate([jnp.full((2,), -1, jnp.int32), id_row[:-2]])
    keep_mask = earlier == id_row
    moved = jnp.concatenate([jnp.zeros((2, width), h_one.dtype), h_one[:-2]], axis=0)
    shifted = jnp.where(keep_mask[:, None], moved, jnp.zeros_like(moved))
    grouped = shifted.reshape(length // 3, 3 * width)
    pooled = low_back(low(product(grouped, pool_weight.T)))
    short_ids = id_row.reshape(length // 3, 3)[:, 0]
    h_three = low_back(low(residual_block(pooled, short_ids, second_block)))
    upsampled = product(h_three, expansion_weight).reshape(length, width)
    return low(upsampled + h_one)

def reference(activations, cotangent, article_ids, section_proj, out_rows, up_rows, down_rows, norm_gains, slopes):
    checked = jax.checkpoint(one_row)

    def forward(acts_f, proj_f, out_f, up_f, down_f, gain_f, slope_f):
        first_block = (proj_f[0], out_f[:D], up_f[:D], down_f[:FF], gain_f[0:2], slope_f[0:2].reshape(-1))
        second_block = (proj_f[2], out_f[D:], up_f[D:], down_f[FF:], gain_f[2:4], slope_f[2:4].reshape(-1))
        weight_set = (first_block, second_block, proj_f[1], proj_f[3])
        flat_acts = acts_f.reshape(-1, L, D)
        flat_ids = article_ids.reshape(-1, L).astype(jnp.int32)

        def run_row(row_pair):
            return checked(weight_set, row_pair[0], row_pair[1])
        rows_out = lax.map(run_row, (flat_acts, flat_ids))
        return rows_out.reshape(acts_f.shape)
    primal, pullback = jax.vjp(forward, activations.astype(jnp.float32), section_proj.astype(jnp.float32), out_rows.astype(jnp.float32), up_rows.astype(jnp.float32), down_rows.astype(jnp.float32), norm_gains.astype(jnp.float32), slopes.astype(jnp.float32))
    grads = pullback(cotangent.astype(jnp.float32))
    return (primal.astype(jnp.bfloat16), grads[0], grads[1], grads[2], grads[3], grads[4], grads[5], grads[6])
```

```python
import functools

import jax
import jax.numpy as jnp
from jax import lax
from jax.experimental import pallas as pl
from jax.experimental.pallas import tpu as pltpu
from jax.sharding import PartitionSpec as P

EPSILON = 1e-05
APART = -1e30
F32 = jnp.float32
BF16 = jnp.bfloat16
VMEM_LIMIT = 60 * 1024 * 1024
LANES = 128
PARTS = 4
HALF = 64
MESH = pl.DeviceIdType.MESH


def dot(left, right, left_dim, right_dim):
    return lax.dot_general(
        left, right, (((left_dim,), (right_dim,)), ((), ())), preferred_element_type=F32
    )


def standardize(value):
    centred = value - jnp.mean(value, axis=-1, keepdims=True)
    inverse = lax.rsqrt(jnp.mean(centred * centred, axis=-1, keepdims=True) + EPSILON)
    return centred * inverse, inverse


def norm_back(grad, gain, standard, inverse):
    scaled = grad * gain
    centred = (
        scaled
        - jnp.mean(scaled, axis=-1, keepdims=True)
        - standard * jnp.mean(scaled * standard, axis=-1, keepdims=True)
    )
    return centred * inverse


def params(limit=VMEM_LIMIT):
    return pltpu.CompilerParams(vmem_limit_bytes=limit)


def row_cuts(length, step):
    return [slice(start, start + step) for start in range(0, length, step)]


def lane_ids(rows):
    return lax.broadcasted_iota(jnp.int32, (rows, LANES), 1)


def barrier_with(devices):
    barrier = pltpu.get_barrier_semaphore()
    for device in devices:
        pl.semaphore_signal(barrier, inc=1, device_id=device, device_id_type=MESH)
    pl.semaphore_wait(barrier, len(devices))


def make_marks(wide, lane):
    length = wide.shape[0]
    mark = lane % HALF
    position = lax.broadcasted_iota(jnp.int32, (length, LANES), 0)
    low = position % 256
    same = wide == (mark - 2).astype(F32)
    chosen = (mark >= 2) & (mark < 5)
    query = jnp.where(chosen & same, 1.0, 0.0)
    fixed = jnp.where(mark < 8, 1.0, 0.0)
    apart = jnp.where(same, 0.0, APART)
    key = jnp.where(chosen, apart, fixed)
    key = jnp.where(mark == 0, low.astype(F32), key)
    key = jnp.where(mark == 1, (position - low).astype(F32), key)
    return query.astype(BF16), key.astype(BF16)


def gelu_pieces(value):
    root = 0.7978845608028654
    square = value * value
    inner = jnp.tanh(value * (root + (root * 0.044715) * square))
    half = 0.5 + 0.5 * inner
    active = value * half
    slant = half + active * (1.0 - inner) * (root + (3.0 * root * 0.044715) * square)
    return active, slant


LINE = 4
SQUARE = 2 * LINE


def head_back(
    side,
    key_mark_ref,
    query_ref,
    key_ref,
    value_ref,
    attended_ref,
    attended_grad_ref,
    mixed,
    keys,
    values,
    grads,
    key_sum,
    value_sum,
    cuts,
    tile,
):
    length = key_ref.shape[0]
    blocks = length // tile
    lane = lane_ids(tile)
    here = lane // HALF == side
    mark = lane % HALF
    earlier = lax.broadcasted_iota(jnp.int32, (tile, tile), 0) <= lax.broadcasted_iota(
        jnp.int32, (tile, tile), 1
    )
    position = lax.broadcasted_iota(jnp.int32, (tile, LANES), 0)
    spans = [slice(block * tile, (block + 1) * tile) for block in range(blocks)]
    for rows in spans:
        grad = attended_grad_ref[rows, :].astype(F32)
        product = jnp.where(here, grad * attended_ref[rows, :].astype(F32), 0.0)
        keys[rows, :] = jnp.where(
            here, key_ref[rows, :].astype(F32), key_mark_ref[rows, :].astype(F32)
        ).astype(BF16)
        values[rows, :] = jnp.where(here, value_ref[rows, :].astype(F32), 1.0).astype(BF16)
        centre = -jnp.sum(product, axis=1, keepdims=True)
        first = centre.astype(BF16).astype(F32)
        second = (centre - first).astype(BF16).astype(F32)
        third = centre - first - second
        marks = jnp.where(
            mark == 0, first, jnp.where(mark == 1, second, jnp.where(mark == 2, third, 0.0))
        )
        grads[rows, :] = jnp.where(here, grad, marks).astype(BF16)

    def score(block, other):
        rows, cols = spans[block], spans[other]
        raw = dot(keys[cols, :], query_ref[0, rows, :], 1, 1)
        return raw, dot(values[cols, :], grads[rows, :], 1, 1)

    def finish(block, other, raw, pull):
        rows, cols = spans[block], spans[other]
        weights = jnp.exp(raw)
        if other == block:
            weights = jnp.where(earlier, weights, 0.0)
        change = (weights * pull).astype(BF16)
        key_term = dot(change, query_ref[0, rows, :], 1, 0)
        value_term = dot(weights.astype(BF16), grads[rows, :], 1, 0)
        if other == block:
            key_sum[cols, :] = key_term
            value_sum[cols, :] = value_term
        else:
            key_sum[cols, :] += key_term
            value_sum[cols, :] += value_term
        return dot(change, keys[cols, :], 0, 0)

    def keep(rows, cut, value):
        mixed[rows, cut] = jnp.where(here, value, mixed[rows, cut].astype(F32)).astype(BF16)

    order = [(block, other) for block in range(blocks) for other in range(block + 1)]
    ahead = score(*order[0])
    slope_sum = jnp.zeros((tile, LANES), F32)
    total = None
    for index, (block, other) in enumerate(order):
        now = ahead
        if index + 1 < len(order):
            ahead = score(*order[index + 1])
        term = finish(block, other, *now)
        total = term if other == 0 else total + term
        if other == block:
            place = -(position + block * tile).astype(F32)
            slope_sum = slope_sum + jnp.where(
                mark < 2, total, jnp.where(mark == 5, total * place, 0.0)
            )
            keep(spans[block], cuts[0], total * 0.125)
    for rows in spans:
        keep(rows, cuts[1], key_sum[rows, :])
        keep(rows, cuts[2], value_sum[rows, :])
    return jnp.sum(jnp.where(here, 0.0, slope_sum))


def head_cuts(pair, width):
    return [
        pl.ds(pl.multiple_of(place * width + pair * LANES, LANES), LANES) for place in range(3)
    ]


def first_kernel(
    act_ref,
    cot_ref,
    ids_ref,
    gain_ref,
    slope_ref,
    proj_src,
    out_src,
    up_src,
    down_src,
    row_dst,
    proj_dst,
    out_dst,
    up_dst,
    down_dst,
    query_dst,
    keyval_dst,
    attended_dst,
    middle_dst,
    active_dst,
    slant_dst,
    grouped_dst,
    long_dst,
    pooled_dst,
    back_dst,
    small_all,
    key_mark,
    short_query_mark,
    short_key_mark,
    keep_ref,
    row_ref,
    proj_all,
    out_all,
    up_all,
    down_all,
    query_mark,
    wide_ref,
    mixed,
    queries,
    keys,
    values,
    attended,
    middle,
    actives,
    slants,
    moved,
    grouped,
    result,
    pooled_own,
    pooled,
    back,
    load_sem,
    row_send,
    row_recv,
    pair_send,
    pair_recv,
    pool_send,
    pool_recv,
    done_sem,
    *,
    tile,
    heads,
):
    section = lax.axis_index("section")
    group = lax.axis_index("dp")
    sections = 4
    core = section % 2
    chip = section // 2
    partner = chip * 2 + (1 - core)
    quarter, width = act_ref.shape[2:]
    length = row_ref.shape[0]
    short = length // 3
    groups = width // LANES
    units = up_all.shape[1]
    piece = units // PARTS
    blocks = length // tile

    def span_of(whole):
        rows = whole.shape[0] // 2
        return pl.ds(pl.multiple_of(core * rows, rows), rows)

    wholes = (proj_all, small_all, out_all, up_all, down_all)
    shards = (proj_src, None, out_src, up_src, down_src)

    def load_copy(index):
        return pltpu.make_async_copy(
            shards[index], wholes[index].at[span_of(wholes[index]), :], load_sem.at[index]
        )

    for index in (0, 2, 3, 4):
        load_copy(index).start()
    small_rows = span_of(small_all)
    small_all[small_rows, :] = jnp.concatenate(
        [
            gain_ref[...].astype(F32),
            jnp.concatenate(
                [
                    slope_ref[...].astype(F32),
                    jnp.zeros((1, width - slope_ref.shape[1]), F32),
                ],
                axis=1,
            ),
            jnp.zeros((6, width), F32),
        ],
        axis=0,
    )
    others = [lax.rem(section + hop, sections) for hop in range(1, sections)]
    barrier_with([(other, group) for other in others])
    place = pl.ds(pl.multiple_of(section * quarter, quarter), quarter)

    def row_copy(source_ref, hop):
        target = lax.rem(section + hop, sections)
        return pltpu.make_async_remote_copy(
            src_ref=source_ref.at[target % 2, 0],
            dst_ref=row_ref.at[place, :],
            send_sem=row_send.at[hop],
            recv_sem=row_recv.at[hop],
            device_id=(target, group),
            device_id_type=MESH,
        )

    for hop in (2, 1, 3):
        target_chip = lax.rem(section + hop, sections) // 2

        @pl.when(target_chip == 0)
        def _():
            row_copy(act_ref, hop).start()

        @pl.when(target_chip == 1)
        def _():
            row_copy(cot_ref, hop).start()

    def pair_copy(index):
        spot = wholes[index].at[span_of(wholes[index]), :]
        return pltpu.make_async_remote_copy(
            src_ref=spot,
            dst_ref=spot,
            send_sem=pair_send.at[index],
            recv_sem=pair_recv.at[index],
            device_id=(partner, group),
            device_id_type=MESH,
        )

    for index in range(len(wholes)):
        if shards[index] is not None:
            load_copy(index).wait()
        pair_copy(index).start()

    @pl.when(chip == 0)
    def _():
        row_ref[place, :] = act_ref[core, 0]

    @pl.when(chip == 1)
    def _():
        row_ref[place, :] = cot_ref[core, 0]

    ids = jnp.broadcast_to(ids_ref[core].astype(F32), (LANES, length))
    wide = ids.T
    wide_ref[0:8, :] = jnp.full((8, LANES), -1.0, F32)
    wide_ref[8:, :] = wide
    query_mark[...], key_mark[...] = make_marks(wide, lane_ids(length))
    short_wide = wide_ref[pl.ds(8, short, stride=3), :]
    short_query_mark[...], short_key_mark[...] = make_marks(short_wide, lane_ids(short))
    for turn in range(3):
        current = wide_ref[pl.ds(8 + turn, short, stride=3), :]
        before = wide_ref[pl.ds(6 + turn, short, stride=3), :]
        keep_ref[turn] = jnp.where(current == before, 1.0, 0.0)
    pair_copy(0).wait_recv()
    pair_copy(1).wait_recv()

    @pl.when(core == 0)
    def _():
        row_copy(act_ref, 3).wait_recv()

    @pl.when(core == 1)
    def _():
        row_copy(act_ref, 1).wait_recv()

    lane = lane_ids(tile)
    upper = lane >= HALF
    mark = lane % HALF
    sides = (jnp.logical_not(upper), upper)
    earlier = lax.broadcasted_iota(jnp.int32, (tile, tile), 0) >= lax.broadcasted_iota(
        jnp.int32, (tile, tile), 1
    )
    spans = [slice(block * tile, (block + 1) * tile) for block in range(blocks)]

    def project(rows):
        standard, _ = standardize(row_ref[rows, :].astype(F32))
        normal = (standard * small_all[0:1, :]).astype(BF16)
        mixed[rows, :] = dot(normal, proj_all[0:width, :], 1, 0).astype(BF16)

    def attend(members):
        def attend_pair(pair, carry):
            cuts = head_cuts(pair, width)
            column = lax.broadcasted_iota(jnp.int32, (1, width), 1)
            per = heads // 2
            slope_of = []
            for side in range(2):
                number = 2 * pair + side
                slopes = jnp.where(number < per, small_all[1:2, :], small_all[9:10, :])
                slope_of.append(
                    jnp.sum(
                        jnp.where(column == number % per, slopes, 0.0), axis=1, keepdims=True
                    )
                )
            for block in members:
                rows = spans[block]
                key_rows = mixed[rows, cuts[1]].astype(F32)
                value_rows = mixed[rows, cuts[2]].astype(F32)
                marks = key_mark[rows, :].astype(F32)
                for side, here in enumerate(sides):
                    keys[2 * pair + side, rows, :] = jnp.where(here, key_rows, marks).astype(BF16)
                    values[2 * pair + side, rows, :] = jnp.where(here, value_rows, 1.0).astype(
                        BF16
                    )

            def score(block, side):
                rows = spans[block]
                marks = jnp.where(mark < 2, slope_of[side], query_mark[rows, :].astype(F32))
                query = jnp.where(sides[side], mixed[rows, cuts[0]].astype(F32) * 0.125, marks)
                query = query.astype(BF16)
                number = 2 * pair + side
                near = jnp.where(earlier, dot(query, keys[number, rows, :], 1, 1), APART)
                far = dot(query, keys[number, : block * tile, :], 1, 1) if block else None
                return query, near, far

            def finish(block, side, query, near, far):
                rows = spans[block]
                number = 2 * pair + side
                highest = jnp.max(near, axis=1, keepdims=True)
                if block:
                    highest = jnp.maximum(highest, jnp.max(far, axis=1, keepdims=True))
                mass = dot(jnp.exp(near - highest).astype(BF16), values[number, rows, :], 1, 0)
                if block:
                    mass = mass + dot(
                        jnp.exp(far - highest).astype(BF16),
                        values[number, : block * tile, :],
                        1,
                        0,
                    )
                level = -(highest + jnp.log(mass))
                first = level.astype(BF16).astype(F32)
                second = (level - first).astype(BF16).astype(F32)
                third = level - first - second
                query = query.astype(F32)
                level_marks = jnp.where(
                    mark == 5,
                    first,
                    jnp.where(mark == 6, second, jnp.where(mark == 7, third, query)),
                )
                queries[number, rows, :] = jnp.where(sides[side], query, level_marks).astype(BF16)
                return mass / pltpu.roll(mass, HALF, 1)

            order = [(block, side) for block in members for side in range(2)]
            ahead = score(*order[0])
            shares = [None, None]
            for index, (block, side) in enumerate(order):
                now = ahead
                if index + 1 < len(order):
                    ahead = score(*order[index + 1])
                shares[side] = finish(block, side, *now)
                if side:
                    attended[spans[block], cuts[0]] = jnp.where(
                        upper, shares[1], shares[0]
                    ).astype(BF16)
            return carry

        lax.fori_loop(0, heads // 2, attend_pair, 0)

    def rows_wait_rest():
        row_copy(act_ref, 2).wait_recv()

        @pl.when(core == 0)
        def _():
            row_copy(act_ref, 1).wait_recv()

        @pl.when(core == 1)
        def _():
            row_copy(act_ref, 3).wait_recv()

    def pool_copy(block):
        rows = pl.ds(block * (tile // 3), tile // 3)
        return pltpu.make_async_remote_copy(
            src_ref=pooled_own.at[rows, :],
            dst_ref=pooled.at[rows, :],
            send_sem=pool_send.at[block],
            recv_sem=pool_recv.at[block],
            device_id=(lax.rem(section + 2, sections), group),
            device_id_type=MESH,
        )

    def out_copies(members=range(6)):
        kept = [
            (proj_all, proj_dst),
            (out_all, out_dst),
            (up_all, up_dst),
            (down_all, down_dst),
            (row_ref, row_dst),
            (grouped, grouped_dst),
        ]
        return [
            pltpu.make_async_copy(*kept[member], done_sem.at[member]) for member in members
        ]

    def attend_copies():
        kept = [
            (queries, query_dst),
            (mixed.at[:, pl.ds(width, 2 * width)], keyval_dst),
            (attended, attended_dst),
        ]
        return [
            pltpu.make_async_copy(origin, target, done_sem.at[6 + index])
            for index, (origin, target) in enumerate(kept)
        ]

    def tile_copies(block):
        rows = pl.ds(block * tile, tile)
        kept = [(middle, middle_dst), (actives, active_dst), (slants, slant_dst), (result, long_dst)]
        return [
            pltpu.make_async_copy(
                origin.at[rows, :], target.at[rows, :], done_sem.at[9 + 4 * block + index]
            )
            for index, (origin, target) in enumerate(kept)
        ]

    @pl.when(chip == 0)
    def _():
        for start in range(0, 2 * quarter, quarter):
            project(slice(start, start + quarter))
        attend((0,))

    rows_wait_rest()
    for index in range(2, len(wholes)):
        pair_copy(index).wait_recv()
    for copy in out_copies(range(5)):
        copy.start()

    @pl.when(chip == 0)
    def _():
        for start in range(2 * quarter, length, quarter):
            project(slice(start, start + quarter))
        attend(tuple(range(1, blocks)))
        for copy in attend_copies():
            copy.start()
        for part in range(groups):
            moved[part, 0:8, :] = jnp.zeros((8, LANES), F32)
        for block, rows in enumerate(spans):
            value = row_ref[rows, :].astype(F32) + dot(attended[rows, :], out_all[...], 1, 0)
            middle[rows, :] = value
            standard, _ = standardize(value)
            normal = (standard * small_all[8:9, :]).astype(BF16)
            for part in range(PARTS):
                span = slice(part * piece, (part + 1) * piece)
                active, slant = gelu_pieces(dot(normal, up_all[:, span], 1, 0))
                active = active.astype(BF16)
                actives[rows, span] = active
                slants[rows, span] = slant.astype(BF16)
                value = value + dot(active, down_all[span, :], 1, 0)
            low = value.astype(BF16)
            result[rows, :] = low
            for copy in tile_copies(block):
                copy.start()
            small_tile = tile // 3
            for part in range(groups):
                lanes = slice(part * LANES, (part + 1) * LANES)
                moved[part, 8 + block * tile : 8 + (block + 1) * tile, :] = low[:, lanes].astype(
                    F32
                )
            total = None
            small_rows = slice(block * small_tile, (block + 1) * small_tile)
            for turn in range(3):
                picked = jnp.concatenate(
                    [
                        moved[part, pl.ds(6 + turn + block * tile, small_tile, stride=3), :]
                        for part in range(groups)
                    ],
                    axis=1,
                )
                factor = jnp.concatenate([keep_ref[turn, small_rows, :]] * groups, axis=1)
                picked = (picked * factor).astype(BF16)
                cut = slice(turn * width, (turn + 1) * width)
                grouped[small_rows, cut] = picked
                term = dot(picked, proj_all[width : 2 * width, cut], 1, 1)
                total = term if total is None else total + term
            pooled_own[small_rows, :] = total.astype(BF16)
            pool_copy(block).start()

    @pl.when(chip == 1)
    def _():
        for part in range(groups):
            lanes = slice(part * LANES, (part + 1) * LANES)
            moved[part, 8:, :] = row_ref[:, lanes].astype(F32)
        for turn in range(3):
            for part in range(groups):
                left = turn * width + part * LANES
                grouped[:, left : left + LANES] = moved[
                    part, pl.ds(8 + turn, short, stride=3), :
                ].astype(BF16)
        back[...] = dot(grouped[...], proj_all[width : 2 * width, :], 1, 1).astype(BF16)
        back_copy = pltpu.make_async_copy(back, back_dst, done_sem.at[21])
        back_copy.start()
        long_copy = pltpu.make_async_copy(row_ref, long_dst, done_sem.at[22])
        long_copy.start()
        back_copy.wait()
        long_copy.wait()
        for block in range(blocks):
            pool_copy(block).wait_recv()
        pooled_copy = pltpu.make_async_copy(pooled, pooled_dst, done_sem.at[23])
        pooled_copy.start()
        pooled_copy.wait()

    out_copies([5])[0].start()

    @pl.when(chip == 0)
    def _():
        for copy in attend_copies():
            copy.wait()
        for block in range(blocks):
            for copy in tile_copies(block):
                copy.wait()
            pool_copy(block).wait_send()

    for copy in out_copies():
        copy.wait()
    for index in range(len(wholes)):
        pair_copy(index).wait_send()
    for hop in range(1, sections):
        row_copy(act_ref, hop).wait_send()


def first_call(
    activations, cotangent, ids, gains, slopes, proj, out_rows, up_rows, down_rows, heads, tile
):
    inside = pl.BlockSpec(memory_space=pltpu.VMEM)
    anywhere = pl.BlockSpec(memory_space=pl.ANY)
    quarter, width = activations.shape[2:]
    length = 4 * quarter
    short = length // 3
    units = up_rows.shape[1]
    shape = jax.ShapeDtypeStruct
    vmem = pltpu.VMEM
    twice = lambda value: (2 * value.shape[0], value.shape[1])
    weights = [twice(value) for value in (proj, out_rows, up_rows, down_rows)]
    return pl.pallas_call(
        functools.partial(first_kernel, tile=tile, heads=heads),
        in_specs=[inside] * 5 + [anywhere] * 4,
        out_specs=[anywhere] * 15 + [inside] * 5,
        out_shape=[shape((length, width), BF16)]
        + [shape(size, BF16) for size in weights]
        + [
            shape((heads, length, LANES), BF16),
            shape((length, 2 * width), BF16),
            shape((length, width), BF16),
            shape((length, width), F32),
            shape((length, units), BF16),
            shape((length, units), BF16),
            shape((short, 3 * width), BF16),
            shape((length, width), BF16),
            shape((short, width), BF16),
            shape((short, width), BF16),
            shape((16, width), F32),
            shape((length, LANES), BF16),
            shape((short, LANES), BF16),
            shape((short, LANES), BF16),
            shape((3, short, LANES), F32),
        ],
        scratch_shapes=[vmem((length, width), BF16)]
        + [vmem(size, BF16) for size in weights]
        + [
            vmem((length, LANES), BF16),
            vmem((length + 8, LANES), F32),
            vmem((length, 3 * width), BF16),
            vmem((heads, length, LANES), BF16),
            vmem((heads, length, LANES), BF16),
            vmem((heads, length, LANES), BF16),
            vmem((length, width), BF16),
            vmem((length, width), F32),
            vmem((length, units), BF16),
            vmem((length, units), BF16),
            vmem((width // LANES, length + 8, LANES), F32),
            vmem((short, 3 * width), BF16),
            vmem((length, width), BF16),
            vmem((short, width), BF16),
            vmem((short, width), BF16),
            vmem((short, width), BF16),
            pltpu.SemaphoreType.DMA((5,)),
            pltpu.SemaphoreType.DMA((4,)),
            pltpu.SemaphoreType.DMA((4,)),
            pltpu.SemaphoreType.DMA((5,)),
            pltpu.SemaphoreType.DMA((5,)),
            pltpu.SemaphoreType.DMA((3,)),
            pltpu.SemaphoreType.DMA((3,)),
            pltpu.SemaphoreType.DMA((24,)),
        ],
        compiler_params=pltpu.CompilerParams(
            collective_id=0, has_side_effects=True, vmem_limit_bytes=VMEM_LIMIT
        ),
        name="first",
    )(activations, cotangent, ids, gains, slopes, proj, out_rows, up_rows, down_rows)


def short_kernel(
    hidden_ref,
    grad_ref,
    gain_ref,
    query_mark_ref,
    key_mark_ref,
    proj_src,
    out_src,
    up_src,
    down_src,
    result_dst,
    hidden_dst,
    even_dst,
    out_dst,
    up_dst,
    down_dst,
    small_ref,
    proj_ref,
    out_ref,
    up_ref,
    down_ref,
    result_ref,
    hidden_grad,
    even_grad,
    out_grad,
    up_grad,
    down_grad,
    mixed,
    queries,
    keys,
    values,
    grads,
    key_sum,
    value_sum,
    attended,
    middle,
    total,
    normal,
    flip,
    grad_flip,
    actives,
    slants,
    attended_grad,
    mixed_grad,
    load_sem,
    done_sem,
    *,
    heads,
):
    length, width = hidden_ref.shape
    units = up_ref.shape[1]
    piece = units // PARTS
    loads = [
        pltpu.make_async_copy(origin, target, load_sem.at[index])
        for index, (origin, target) in enumerate(
            (
                (proj_src.at[0:width, :], proj_ref),
                (out_src, out_ref),
                (up_src, up_ref),
                (down_src, down_ref),
            )
        )
    ]
    for copy in loads:
        copy.start()
    lane = lane_ids(length)
    upper = lane >= HALF
    mark = lane % HALF
    earlier = lax.broadcasted_iota(jnp.int32, (length, length), 0) >= lax.broadcasted_iota(
        jnp.int32, (length, length), 1
    )
    standard, _ = standardize(hidden_ref[...].astype(F32))
    low = (standard * gain_ref[0:1, :]).astype(BF16)
    flip[...] = low.T
    loads[0].wait()
    mixed[...] = dot(low, proj_ref[...], 1, 0).astype(BF16)
    small_ref[...] = jnp.zeros_like(small_ref)
    column = lax.broadcasted_iota(jnp.int32, (1, width), 1)
    sides = (jnp.logical_not(upper), upper)
    per = heads // 2

    def attend_pair(pair, carry):
        cuts = head_cuts(pair, width)
        query_rows = mixed[:, cuts[0]].astype(F32) * 0.125
        key_rows = mixed[:, cuts[1]].astype(F32)
        value_rows = mixed[:, cuts[2]].astype(F32)
        scores, parts = [], []
        for side, here in enumerate(sides):
            number = 2 * pair + side
            slopes = jnp.where(number < per, gain_ref[1:2, :], gain_ref[9:10, :])
            slope = jnp.sum(jnp.where(column == number % per, slopes, 0.0), axis=1, keepdims=True)
            keys[side] = jnp.where(here, key_rows, key_mark_ref[...].astype(F32)).astype(BF16)
            values[side] = jnp.where(here, value_rows, 1.0).astype(BF16)
            marks = jnp.where(mark < 2, slope, query_mark_ref[...].astype(F32))
            query = jnp.where(here, query_rows, marks).astype(BF16)
            parts.append(query)
            scores.append(jnp.where(earlier, dot(query, keys[side], 1, 1), APART))
        shares = []
        for side, here in enumerate(sides):
            highest = jnp.max(scores[side], axis=1, keepdims=True)
            mass = dot(jnp.exp(scores[side] - highest).astype(BF16), values[side], 1, 0)
            level = -(highest + jnp.log(mass))
            first = level.astype(BF16).astype(F32)
            second = (level - first).astype(BF16).astype(F32)
            third = level - first - second
            query = parts[side].astype(F32)
            level_marks = jnp.where(
                mark == 5, first, jnp.where(mark == 6, second, jnp.where(mark == 7, third, query))
            )
            queries[2 * pair + side] = jnp.where(here, query, level_marks).astype(BF16)
            shares.append(mass / pltpu.roll(mass, HALF, 1))
        attended[:, cuts[0]] = jnp.where(upper, shares[1], shares[0]).astype(BF16)
        return carry

    lax.fori_loop(0, heads // 2, attend_pair, 0)
    loads[1].wait()
    value = hidden_ref[...].astype(F32) + dot(attended[...], out_ref[...], 1, 0)
    middle[...] = value
    total[...] = value
    standard, _ = standardize(value)
    normal[...] = (standard * gain_ref[8:9, :]).astype(BF16)
    loads[2].wait()
    loads[3].wait()
    for part in range(PARTS):
        span = slice(part * piece, (part + 1) * piece)
        raised = dot(normal[...], up_ref[:, span], 1, 0)
        active, slant = gelu_pieces(raised)
        active = active.astype(BF16)
        actives[:, span] = active
        slants[:, span] = slant.astype(BF16)
        total[...] += dot(active, down_ref[span, :], 1, 0)
    result_ref[...] = total[...].astype(BF16)
    results = [pltpu.make_async_copy(result_ref, result_dst, done_sem.at[0])]
    results[0].start()

    grad_flip[...] = grad_ref[...].T
    normal_flip = normal[...].T
    for part in range(PARTS):
        span = slice(part * piece, (part + 1) * piece)
        down_grad[span, :] = dot(grad_flip[...], actives[:, span], 1, 0).astype(BF16).T
        grad_active = dot(grad_ref[...], down_ref[span, :], 1, 1)
        low = (grad_active * slants[:, span].astype(F32)).astype(BF16)
        term = dot(low, up_ref[:, span], 1, 1)
        if part:
            total[...] += term
        else:
            total[...] = term
        up_grad[:, span] = dot(normal_flip, low, 1, 0).astype(BF16)
    for index, (origin, target) in enumerate(((down_grad, down_dst), (up_grad, up_dst))):
        results.append(pltpu.make_async_copy(origin, target, done_sem.at[1 + index]))
        results[-1].start()
    standard, inverse = standardize(middle[...])
    grad = total[...]
    small_ref[1:2, :] = jnp.sum(grad * standard, axis=0, keepdims=True)
    middle_grad = grad_ref[...].astype(F32) + norm_back(grad, gain_ref[8:9, :], standard, inverse)
    total[...] = middle_grad
    low = middle_grad.astype(BF16)
    attended_grad[...] = dot(low, out_ref[...], 1, 1).astype(BF16)
    out_grad[...] = dot(attended[...], low, 0, 0).astype(BF16)
    results.append(pltpu.make_async_copy(out_grad, out_dst, done_sem.at[3]))
    results[-1].start()

    def back_pair(pair, carry):
        cuts = head_cuts(pair, width)
        for side in range(2):
            slope_grad = head_back(
                side, key_mark_ref, queries.at[pl.ds(2 * pair + side, 1)], mixed.at[:, cuts[1]],
                mixed.at[:, cuts[2]], attended.at[:, cuts[0]], attended_grad.at[:, cuts[0]],
                mixed_grad, keys.at[side], values.at[side], grads.at[side], key_sum.at[side],
                value_sum.at[side], cuts, length,
            )
            small_ref[2:3, :] += jnp.where(column == 2 * pair + side, slope_grad, 0.0)
        return carry

    lax.fori_loop(0, heads // 2, back_pair, 0)
    for place in range(3):
        span = slice(place * width, (place + 1) * width)
        even_grad[:, span] = dot(flip[...], mixed_grad[:, span], 1, 0).astype(BF16)
    results.append(pltpu.make_async_copy(even_grad, even_dst, done_sem.at[4]))
    results[-1].start()
    standard, inverse = standardize(hidden_ref[...].astype(F32))
    grad = dot(mixed_grad[...], proj_ref[...], 1, 1)
    small_ref[0:1, :] = jnp.sum(grad * standard, axis=0, keepdims=True)
    hidden_grad[...] = (
        total[...] + norm_back(grad, gain_ref[0:1, :], standard, inverse)
    ).astype(BF16)
    results.append(pltpu.make_async_copy(hidden_grad, hidden_dst, done_sem.at[5]))
    results[-1].start()
    for copy in results:
        copy.wait()


def short_call(
    hidden, grad, gains, query_mark, key_mark, proj, out_weight, up_weight, down_weight, heads
):
    inside = pl.BlockSpec(memory_space=pltpu.VMEM)
    anywhere = pl.BlockSpec(memory_space=pl.ANY)
    length, width = hidden.shape
    units = up_weight.shape[1]
    vmem = pltpu.VMEM
    shape = jax.ShapeDtypeStruct
    grads = [(width, 3 * width), out_weight.shape, up_weight.shape, down_weight.shape]
    return pl.pallas_call(
        functools.partial(short_kernel, heads=heads),
        in_specs=[inside] * 5 + [anywhere] * 4,
        out_specs=[anywhere] * 6 + [inside],
        out_shape=[shape((length, width), BF16)] * 2
        + [shape(size, BF16) for size in grads]
        + [shape((8, width), F32)],
        scratch_shapes=[
            vmem((width, 3 * width), BF16),
            vmem(out_weight.shape, BF16),
            vmem(up_weight.shape, BF16),
            vmem(down_weight.shape, BF16),
            vmem((length, width), BF16),
            vmem((length, width), BF16),
        ]
        + [vmem(size, BF16) for size in grads]
        + [
            vmem((length, 3 * width), BF16),
            vmem((heads, length, LANES), BF16),
            vmem((2, length, LANES), BF16),
            vmem((2, length, LANES), BF16),
            vmem((2, length, LANES), BF16),
            vmem((2, length, LANES), F32),
            vmem((2, length, LANES), F32),
            vmem((length, width), BF16),
            vmem((length, width), F32),
            vmem((length, width), F32),
            vmem((length, width), BF16),
            vmem((width, length), BF16),
            vmem((width, length), BF16),
            vmem((length, units), BF16),
            vmem((length, units), BF16),
            vmem((length, width), BF16),
            vmem((length, 3 * width), BF16),
            pltpu.SemaphoreType.DMA((4,)),
            pltpu.SemaphoreType.DMA((6,)),
        ],
        compiler_params=params(),
        name="short",
    )(hidden, grad, gains, query_mark, key_mark, proj, out_weight, up_weight, down_weight)


def chunk_list():
    chunks = [("odd", 1, 0, 512, place * 512, 512) for place in range(3)]
    chunks += [("up", None, 0, 256, place * 512, 512) for place in (0, 2)]
    chunks += [("down", None, 0, 512, 0, 512)]
    chunks += [("up", None, 0, 256, place * 512, 512) for place in (1, 3)]
    chunks += [("down", None, 512, 512, 0, 512)]
    chunks += [("out", None, 0, 256, 0, 512)]
    chunks += [("even", 0, 0, 512, pair * 384, 384) for pair in range(4)]
    return chunks


BEGINS = {1: (3,), 2: (4, 5), 3: (6,), 4: (7, 8, 9), 6: (10,), 8: (11,), 10: (12,), 12: (13,)}
TICKS = {
    3: [
        ("pair", 3), ("side", 1), ("side", 2), ("line", 0),
    ],
    4: [
        ("pair", 5), ("side", 3), ("line", 1), ("line", 2), ("side", 4),
    ],
    5: [
        ("line", 3), ("side", 5),
    ],
    6: [
        ("back", 1), ("side", 6), ("pair", 7), ("pair", 9), ("back", 2), ("pair", 8),
        ("full", 0), ("line", 4),
    ],
    7: [
        ("full", 1), ("back", 3), ("side", 7),
    ],
    8: [
        ("pair", 10), ("side", 9), ("line", 5), ("full", 2), ("line", 6),
    ],
    9: [
        ("back", 4), ("side", 8),
    ],
    10: [
        ("line", 7), ("pair", 11), ("full", 3), ("line", 9), ("side", 10),
    ],
    11: [
        ("full", 4), ("back", 5), ("side", 11),
    ],
    12: [
        ("back", 6), ("pair", 12),
    ],
    13: [
        ("line", 8), ("full", 5),
    ],
}
MIDDLES = {
    1: [
        ("pair", 0), ("pair", 1), ("pair", 2),
    ],
    2: [
        ("side", 0),
    ],
    3: [
        ("pair", 4),
    ],
    4: [
        ("pair", 6), ("back", 0),
    ],
}
DRAIN = [
    ("full", 6), ("back", 7), ("pair", 13), ("side", 12), ("back", 9), ("line", 10),
    ("line", 11), ("full", 7), ("side", 13), ("back", 8), ("full", 9), ("line", 12),
    ("back", 10), ("back", 11), ("full", 8), ("line", 13), ("full", 10), ("back", 12),
    ("full", 11), ("back", 13), ("full", 12), ("full", 13),
]


def last_kernel(
    hidden_src,
    gain_ref,
    proj_ref,
    key_mark_src,
    middle_src,
    attended_src,
    out_weight_src,
    keep_ref,
    grouped_ref,
    added_ref,
    active_ref,
    slant_ref,
    up_weight_ref,
    down_weight_ref,
    query_ref,
    key_ref,
    value_ref,
    pooled_grad_ref,
    short_result_ref,
    even_ref,
    out_ref,
    up_ref,
    down_ref,
    small_ref,
    proj_result,
    out_result,
    up_result,
    down_result,
    small_result,
    parts_result,
    middle_ref,
    attended_ref,
    out_weight_ref,
    hidden_ref,
    key_mark_ref,
    short_rows,
    sent_rows,
    moved,
    rows_buf,
    normal,
    grad_flip,
    total,
    lower,
    attended_grad,
    mixed,
    keys,
    values,
    grads,
    key_sum,
    value_sum,
    even_grad,
    odd_grad,
    out_grad,
    up_grad,
    down_grad,
    small_grad,
    small_full,
    parts_ref,
    proj_full,
    out_full,
    up_full,
    down_full,
    proj_pair,
    out_pair,
    up_pair,
    down_pair,
    proj_side,
    out_side,
    up_side,
    down_side,
    proj_line,
    out_line,
    up_line,
    down_line,
    small_pair,
    small_side,
    small_line,
    local_sem,
    pair_send,
    pair_recv,
    side_send,
    side_recv,
    line_send,
    line_recv,
    back_send,
    back_recv,
    full_send,
    full_recv,
    small_send,
    small_recv,
    rows_send,
    rows_recv,
    result_sem,
    load_sem,
    short_send,
    short_recv,
    *,
    tile,
):
    step = pl.program_id(0)
    last = pl.num_programs(0) - 1
    section = lax.axis_index("section")
    group = lax.axis_index("dp")
    core = section % 2
    chip = section // 2
    partner = (chip * 2 + (1 - core), group)
    base = group // SQUARE * SQUARE
    side = group % 2
    line = group % SQUARE // 2
    neighbour = (section, base + line * 2 + (1 - side))
    length, width = hidden_ref.shape
    short = length // 3
    groups = width // LANES
    stride = min(length // 2, 384)
    quarter = parts_ref.shape[1]
    chunks = chunk_list()
    first_head = 1 + PARTS

    def along(hop):
        return (section, base + lax.rem(line + hop, LINE) * 2 + side)

    def across(hop):
        return lax.rem(section + hop, 4)

    source = {"odd": odd_grad, "even": even_grad, "out": out_grad, "up": up_grad, "down": down_grad}
    table = lambda proj, out, up, down: {
        "odd": proj, "even": proj, "out": out, "up": up, "down": down
    }
    sums = table(proj_pair, out_pair, up_pair, down_pair)
    sides = table(proj_side, out_side, up_side, down_side)
    lines = table(proj_line, out_line, up_line, down_line)
    fulls = table(proj_full, out_full, up_full, down_full)
    outcomes = table(proj_result, out_result, up_result, down_result)

    def cut(start, size):
        return pl.ds(pl.multiple_of(start, 16), size)

    def remote(origin, target, send, recv, device):
        return pltpu.make_async_remote_copy(
            src_ref=origin,
            dst_ref=target,
            send_sem=send,
            recv_sem=recv,
            device_id=device,
            device_id_type=MESH,
        )

    def pair_copy(index):
        name, owner, start, rows, left, cols = chunks[index]
        offset = 0 if owner is not None else (1 - core) * (source[name].shape[0] // 2)
        lanes = pl.ds(left, cols)
        return remote(
            source[name].at[cut(offset + start, rows), lanes],
            sums[name].at[cut(start, rows), lanes],
            pair_send.at[index],
            pair_recv.at[index],
            partner,
        )

    def side_copy(index):
        name, _, start, rows, left, cols = chunks[index]
        half = rows // 2
        lanes = pl.ds(left, cols)
        return remote(
            sums[name].at[cut(start + (1 - side) * half, half), lanes],
            sides[name].at[cut(start // 2, half), lanes],
            side_send.at[index],
            side_recv.at[index],
            neighbour,
        )

    def line_copy(index, hop):
        name, _, start, rows, left, cols = chunks[index]
        half, piece = rows // 2, rows // SQUARE
        lanes = pl.ds(left, cols)
        target = lax.rem(line + hop, LINE)
        return remote(
            sums[name].at[cut(start + side * half + target * piece, piece), lanes],
            lines[name].at[hop - 1, cut(start // SQUARE, piece), lanes],
            line_send.at[index, hop - 1],
            line_recv.at[index, hop - 1],
            along(hop),
        )

    def back_copy(index, hop):
        name, _, start, rows, left, cols = chunks[index]
        half, piece = rows // 2, rows // SQUARE
        place = fulls[name].at[
            cut(start + side * half + line * piece, piece), pl.ds(left, cols)
        ]
        return remote(
            place, place, back_send.at[index, hop - 1], back_recv.at[index, hop - 1], along(hop)
        )

    def full_copy(index):
        name, _, start, rows, left, cols = chunks[index]
        half = rows // 2
        place = fulls[name].at[cut(start + side * half, half), pl.ds(left, cols)]
        return remote(place, place, full_send.at[index], full_recv.at[index], neighbour)

    def result_copies(index):
        name, _, start, rows, left, cols = chunks[index]
        spans = [(pl.ds(left, cols), pl.ds(left, cols))]
        if name == "even":
            spans = [span for span in regroup() if left <= span[1].start < left + cols]
        return [
            pltpu.make_async_copy(
                fulls[name].at[cut(start, rows), held],
                outcomes[name].at[cut(start, rows), final],
                result_sem.at[index, number],
            )
            for number, (final, held) in enumerate(spans)
        ]

    def owned(index, act):
        owner = chunks[index][1]
        if owner is None:
            act()
        else:
            pl.when(core == owner)(act)

    def pair_start(index):
        owner = chunks[index][1]
        begin = lambda: pair_copy(index).start()
        if owner is None:
            begin()
        else:
            pl.when(core != owner)(begin)

    def pair_stage(index):
        name, owner, start, rows, left, cols = chunks[index]
        lanes = slice(left, left + cols)
        here = cut(start, rows)

        def act():
            pair_copy(index).wait_recv()
            offset = 0 if owner is not None else core * (source[name].shape[0] // 2)
            mine = source[name][cut(offset + start, rows), lanes].astype(F32)
            arrived = sums[name][here, lanes].astype(F32)
            sums[name][here, lanes] = (mine + arrived).astype(BF16)
            side_copy(index).start()

        if owner is None:
            pair_copy(index).wait_send()
        else:
            pl.when(core != owner)(lambda: pair_copy(index).wait_send())
        owned(index, act)

    def side_stage(index):
        name, _, start, rows, left, cols = chunks[index]
        half = rows // 2
        lanes = slice(left, left + cols)

        def act():
            side_copy(index).wait()
            here = cut(start + side * half, half)
            arrived = sides[name][cut(start // 2, half), lanes].astype(F32)
            sums[name][here, lanes] = (sums[name][here, lanes].astype(F32) + arrived).astype(BF16)
            for hop in range(1, LINE):
                line_copy(index, hop).start()

        owned(index, act)

    def line_stage(index):
        name, _, start, rows, left, cols = chunks[index]
        half, piece = rows // 2, rows // SQUARE
        lanes = slice(left, left + cols)

        def act():
            for hop in range(1, LINE):
                line_copy(index, hop).wait()
            here = cut(start + side * half + line * piece, piece)
            value = sums[name][here, lanes].astype(F32)
            for hop in range(1, LINE):
                value = value + lines[name][hop - 1, cut(start // SQUARE, piece), lanes].astype(F32)
            fulls[name][here, lanes] = value.astype(BF16)
            for hop in range(1, LINE):
                back_copy(index, hop).start()

        owned(index, act)

    def back_stage(index):
        def act():
            for hop in range(1, LINE):
                back_copy(index, hop).wait()
            full_copy(index).start()

        owned(index, act)

    def full_stage(index):
        def act():
            full_copy(index).wait()
            for copy in result_copies(index):
                copy.start()

        owned(index, act)

    def result_wait(index):
        for copy in result_copies(index):
            copy.wait()

    stages = {
        "pair": pair_stage,
        "side": side_stage,
        "line": line_stage,
        "back": back_stage,
        "full": full_stage,
    }

    def rows_copy(hop):
        target = across(hop)
        return remote(
            rows_buf.at[cut(target * quarter, quarter), :],
            parts_ref.at[section],
            rows_send.at[hop],
            rows_recv.at[hop],
            (target, group),
        )

    def load_copies():
        pairs = [
            (out_ref, out_grad),
            (up_ref, up_grad),
            (down_ref, down_grad),
            (small_ref, small_grad),
        ]
        pairs += [
            (even_ref.at[:, origin], even_grad.at[:, target]) for origin, target in regroup()
        ]
        return [
            pltpu.make_async_copy(origin, target, load_sem.at[index])
            for index, (origin, target) in enumerate(pairs)
        ]

    def regroup():
        for pair in range(width // LANES):
            for place in range(3):
                yield (
                    pl.ds(place * width + pair * LANES, LANES),
                    pl.ds((3 * pair + place) * LANES, LANES),
                )

    def kept_copies(members=range(5)):
        pairs = (
            (middle_src, middle_ref),
            (attended_src, attended_ref),
            (out_weight_src, out_weight_ref),
            (hidden_src, hidden_ref),
            (key_mark_src, key_mark_ref),
        )
        return [
            pltpu.make_async_copy(*pairs[member], local_sem.at[1 + member]) for member in members
        ]

    def kept_wait(*members):
        for copy in kept_copies(members):
            copy.wait()

    @pl.when(step == 0)
    def _():
        @pl.when(chip == 0)
        def _():
            for copy in kept_copies():
                copy.start()
            small_grad[...] = jnp.zeros_like(small_grad)

        @pl.when(chip == 1)
        def _():
            pltpu.make_async_copy(pooled_grad_ref, sent_rows, local_sem.at[0]).start()
            pltpu.make_async_copy(short_result_ref, short_rows, local_sem.at[6]).start()
            for copy in load_copies():
                copy.start()

        barrier_with(
            [(across(hop), group) for hop in range(1, 4)]
            + [neighbour]
            + [along(hop) for hop in range(1, LINE)]
        )
        short_copy = remote(
            sent_rows, short_rows, short_send.at[0], short_recv.at[0], (across(2), group)
        )

        @pl.when(chip == 0)
        def _():
            short_copy.wait_recv()

        @pl.when(chip == 1)
        def _():
            pltpu.make_async_copy(pooled_grad_ref, sent_rows, local_sem.at[0]).wait()
            short_copy.start()
            pltpu.make_async_copy(short_result_ref, short_rows, local_sem.at[6]).wait()

        rows = short_rows[...]
        flip = rows.T
        for place in range(3):
            lanes = slice(place * width, (place + 1) * width)
            odd_grad[:, lanes] = dot(flip, grouped_ref[:, lanes], 1, 0).astype(BF16)
            pair_start(place)
        for place in range(3):
            lanes = slice(place * width, (place + 1) * width)
            spread_rows = dot(rows, proj_ref[width : 2 * width, lanes], 1, 0)
            factor = jnp.maximum(keep_ref[place], chip.astype(F32))
            for part in range(groups):
                moved[part, pl.ds(place, short, stride=3), :] = (
                    spread_rows[:, part * LANES : (part + 1) * LANES] * factor
                )
        for part in range(groups):
            lanes = slice(part * LANES, (part + 1) * LANES)
            moved[part, length:, :] = jnp.zeros((8, LANES), F32)
            added = added_ref[:, lanes].astype(F32)

            @pl.when(chip == 0)
            def _():
                rows_buf[:, lanes] = (added + moved[part, 2 : 2 + length, :]).astype(BF16)

            @pl.when(chip == 1)
            def _():
                rows_buf[:, lanes] = (added + moved[part, 0:length, :]).astype(BF16)

        @pl.when(chip == 1)
        def _():
            for copy in load_copies():
                copy.wait()
            short_copy.wait_send()

    for tick, events in TICKS.items():

        @pl.when(step == tick)
        def _():
            for stage, index in events:
                stages[stage](index)

    @pl.when((chip == 0) & (step == 1))
    def _():
        kept_wait(0)
        for rows in row_cuts(length, stride):
            standard, _ = standardize(middle_ref[rows, :])
            normal[:, rows] = (standard * gain_ref[8:9, :]).astype(BF16).T
            grad_flip[:, rows] = rows_buf[rows, :].T
            total[rows, :] = jnp.zeros((stride, width), F32)

    @pl.when((chip == 0) & (step >= 1) & (step < first_head))
    def _():
        turn = step - 1
        part = (turn % 2) * 2 + turn // 2
        span = pl.ds(pl.multiple_of(part * 512, 512), 512)
        down_grad[span, :] = dot(grad_flip[...], active_ref[...], 1, 0).astype(BF16).T

    for tick, events in MIDDLES.items():

        @pl.when(step == tick)
        def _():
            for stage, index in events:
                stages[stage](index)

    @pl.when((chip == 0) & (step >= 1) & (step < first_head))
    def _():
        turn = step - 1
        part = (turn % 2) * 2 + turn // 2
        span = pl.ds(pl.multiple_of(part * 512, 512), 512)
        for rows in row_cuts(length, stride):
            grad_active = dot(rows_buf[rows, :], down_weight_ref[...], 1, 1)
            low = (grad_active * slant_ref[rows, :].astype(F32)).astype(BF16)
            lower[rows, :] = low
            total[rows, :] += dot(low, up_weight_ref[...], 1, 1)
        up_grad[:, span] = dot(normal[...], lower[...], 1, 0).astype(BF16)

    @pl.when((chip == 0) & (step == first_head - 1))
    def _():
        kept_wait(1, 2)
        gain_sum = jnp.zeros((1, width), F32)
        for rows in row_cuts(length, stride):
            standard, inverse = standardize(middle_ref[rows, :])
            grad = total[rows, :]
            gain_sum = gain_sum + jnp.sum(grad * standard, axis=0, keepdims=True)
            middle_grad = rows_buf[rows, :].astype(F32) + norm_back(
                grad, gain_ref[8:9, :], standard, inverse
            )
            total[rows, :] = middle_grad
            low = middle_grad.astype(BF16)
            lower[rows, :] = low
            attended_grad[rows, :] = dot(low, out_weight_ref[...], 1, 1).astype(BF16)
        small_grad[1:2, :] = gain_sum
        out_grad[...] = dot(attended_ref[...], lower[...], 0, 0).astype(BF16)

    @pl.when((chip == 0) & (step == first_head))
    def _():
        kept_wait(3, 4)
        for rows in row_cuts(length, stride):
            standard, _ = standardize(hidden_ref[rows, :].astype(F32))
            normal[:, rows] = (standard * gain_ref[0:1, :]).astype(BF16).T

    @pl.when((chip == 0) & (step >= first_head) & (step < last))
    def _():
        head = step - first_head
        cuts = head_cuts(head // 2, width)
        slope_grad = head_back(
            head % 2, key_mark_ref, query_ref, key_ref, value_ref, attended_ref.at[:, cuts[0]],
            attended_grad.at[:, cuts[0]], mixed, keys, values, grads, key_sum, value_sum,
            cuts, tile,
        )
        column = lax.broadcasted_iota(jnp.int32, (1, width), 1)
        small_grad[2:3, :] += jnp.where(column == head, slope_grad, 0.0)

    @pl.when((chip == 0) & (step >= first_head) & (step < last) & (step % 2 == 0))
    def _():
        pair = (step - first_head) // 2
        for place, span in enumerate(head_cuts(pair, width)):
            target = pl.ds(pl.multiple_of((3 * pair + place) * LANES, LANES), LANES)
            even_grad[:, target] = dot(normal[...], mixed[:, span], 1, 0).astype(BF16)

    for begin, members in BEGINS.items():
        @pl.when(step == begin)
        def _():
            for index in members:
                pair_start(index)

    @pl.when((chip == 0) & (step == last))
    def _():
        gain_sum = jnp.zeros((1, width), F32)
        for rows in row_cuts(length, stride):
            standard, inverse = standardize(hidden_ref[rows, :].astype(F32))
            grad = dot(mixed[rows, :], proj_ref[0:width, :], 1, 1)
            gain_sum = gain_sum + jnp.sum(grad * standard, axis=0, keepdims=True)
            rows_buf[rows, :] = (
                total[rows, :] + norm_back(grad, gain_ref[0:1, :], standard, inverse)
            ).astype(BF16)
        small_grad[0:1, :] = gain_sum

    @pl.when(step == last)
    def _():
        small_one = remote(small_grad, small_pair, small_send.at[0], small_recv.at[0], partner)
        small_one.start()
        for hop in range(1, 4):
            rows_copy(hop).start()
        parts_ref[section] = rows_buf[cut(section * quarter, quarter), :]
        for stage, index in DRAIN[:3]:
            stages[stage](index)
        small_one.wait()
        small_full[...] = small_grad[...] + small_pair[...]
        small_two = remote(small_full, small_side, small_send.at[1], small_recv.at[1], neighbour)
        small_two.start()
        for stage, index in DRAIN[3:7]:
            stages[stage](index)
        small_two.wait()
        small_full[...] = small_full[...] + small_side[...]
        small_rest = [
            remote(
                small_full,
                small_line.at[line],
                small_send.at[1 + hop],
                small_recv.at[1 + hop],
                along(hop),
            )
            for hop in range(1, LINE)
        ]
        for copy in small_rest:
            copy.start()
        for stage, index in DRAIN[7:]:
            stages[stage](index)
        for copy in small_rest:
            copy.wait()
        small_line[line] = small_full[...]
        small_result[...] = (small_line[0] + small_line[1]) + (small_line[2] + small_line[3])
        for hop in range(1, 4):
            rows_copy(hop).wait()
        parts_copy = pltpu.make_async_copy(parts_ref, parts_result, result_sem.at[len(chunks), 0])
        parts_copy.start()
        for index in range(len(chunks)):
            owned(index, functools.partial(result_wait, index))
        parts_copy.wait()


def last_call(
    hidden, gains, proj, key_mark, middle, attended, out_weight, keep, grouped, added,
    active, slant, up_weight, down_weight, query, keyval,
    pooled_grad, short_result, even, out_grad, up_grad, down_grad, small, tile,
):
    inside = pl.BlockSpec(memory_space=pltpu.VMEM)
    anywhere = pl.BlockSpec(memory_space=pl.ANY)
    length, width = hidden.shape
    short = length // 3
    heads = query.shape[0]
    units = up_weight.shape[1]
    wide = even.shape[1]
    piece = units // PARTS
    half = lambda value: (value.shape[0] // 2, value.shape[1])
    shapes = [even.shape, half(out_grad), half(up_grad), half(down_grad)]
    count = len(chunk_list())
    vmem = pltpu.VMEM
    scaled = lambda over: [vmem((rows // over, cols), BF16) for rows, cols in shapes]
    semaphores = lambda *shape: [pltpu.SemaphoreType.DMA(shape)] * 2

    def part_of(step):
        turn = jnp.clip(step - 1, 0, PARTS - 1)
        return turn % 2 * 2 + turn // 2

    def head_of(step):
        return jnp.clip(step - 1 - PARTS, 0, heads - 1)

    column = lambda start: pl.BlockSpec(
        (length, LANES), lambda step: (0, start + head_of(step) // 2)
    )
    results = pl.pallas_call(
        functools.partial(last_kernel, tile=tile),
        grid=(2 + PARTS + heads,),
        in_specs=[anywhere, inside, inside] + [anywhere] * 4 + [inside] * 3
        + [pl.BlockSpec((length, piece), lambda step: (0, part_of(step)))] * 2
        + [
            pl.BlockSpec((width, piece), lambda step: (0, part_of(step))),
            pl.BlockSpec((piece, width), lambda step: (part_of(step), 0)),
            pl.BlockSpec((1, length, LANES), lambda step: (head_of(step), 0, 0)),
            column(0),
            column(heads // 2),
        ]
        + [anywhere] * 7,
        out_specs=[anywhere] * 4 + [inside, anywhere],
        out_shape=[jax.ShapeDtypeStruct(shape, BF16) for shape in shapes]
        + [
            jax.ShapeDtypeStruct(small.shape, F32),
            jax.ShapeDtypeStruct((4, length // 4, width), BF16),
        ],
        scratch_shapes=[
            vmem((length, width), F32),
            vmem((length, width), BF16),
            vmem((width, width), BF16),
            vmem((length, width), BF16),
            vmem((length, LANES), BF16),
            vmem((short, width), BF16),
            vmem((short, width), BF16),
            vmem((width // LANES, length + 8, LANES), F32),
            vmem((length, width), BF16),
            vmem((width, length), BF16),
            vmem((width, length), BF16),
            vmem((length, width), F32),
            vmem((length, width), BF16),
            vmem((length, width), BF16),
            vmem((length, 3 * width), BF16),
            vmem((length, LANES), BF16),
            vmem((length, LANES), BF16),
            vmem((length, LANES), BF16),
            vmem((length, LANES), F32),
            vmem((length, LANES), F32),
            vmem((width, wide), BF16),
            vmem((width, wide), BF16),
            vmem(out_grad.shape, BF16),
            vmem(up_grad.shape, BF16),
            vmem(down_grad.shape, BF16),
            vmem(small.shape, F32),
            vmem(small.shape, F32),
            vmem((4, length // 4, width), BF16),
        ]
        + scaled(1)
        + scaled(1)
        + scaled(2)
        + [vmem((LINE - 1, rows // SQUARE, cols), BF16) for rows, cols in shapes]
        + [vmem(small.shape, F32)] * 2
        + [vmem((LINE,) + small.shape, F32)]
        + [pltpu.SemaphoreType.DMA((7,))]
        + semaphores(count)
        + semaphores(count)
        + semaphores(count, LINE - 1)
        + semaphores(count, LINE - 1)
        + semaphores(count)
        + semaphores(2 + LINE - 1)
        + semaphores(4)
        + [pltpu.SemaphoreType.DMA((count + 1, 3)), pltpu.SemaphoreType.DMA((16,))]
        + semaphores(1),
        compiler_params=pltpu.CompilerParams(
            collective_id=1, has_side_effects=True, vmem_limit_bytes=VMEM_LIMIT
        ),
        name="last",
    )(
        hidden, gains, proj, key_mark, middle, attended, out_weight, keep, grouped, added,
        active, slant, up_weight, down_weight, query, keyval, keyval,
        pooled_grad, short_result, even, out_grad, up_grad, down_grad, small,
    )
    parts = results[-1]
    results = results[:-1]
    squares = lax.axis_size("dp") // SQUARE
    if squares > 1:
        members = [
            [number * SQUARE + place for number in range(squares)] for place in range(SQUARE)
        ]
        results = lax.psum(results, "dp", axis_index_groups=members)
    return results, parts


def widen_kernel(*refs):
    step = pl.program_id(0)
    half = pl.num_programs(0) // 2
    *sources, parts_ref = refs[: len(refs) // 2]
    *targets, input_ref, results_ref = refs[len(refs) // 2 :]
    for source, target in zip(sources, targets):
        target[...] = source[...].astype(F32)

    @pl.when(step < half)
    def _():
        input_ref[...] = parts_ref[...].astype(F32)

    @pl.when(step >= half)
    def _():
        results_ref[...] = parts_ref[...]


def widen_call(grads, parts):
    steps = parts.shape[0]
    half = steps // 2
    block = lambda value: pl.BlockSpec(
        (value.shape[0] // steps, value.shape[1]), lambda step: (step, 0)
    )
    page = (1,) + parts.shape[1:]
    return pl.pallas_call(
        widen_kernel,
        grid=(steps,),
        in_specs=[block(value) for value in grads]
        + [pl.BlockSpec(page, lambda step: (step, 0, 0))],
        out_specs=[block(value) for value in grads]
        + [
            pl.BlockSpec(page, lambda step: (jnp.minimum(step, half - 1), 0, 0)),
            pl.BlockSpec(page, lambda step: (jnp.maximum(step - half, 0), 0, 0)),
        ],
        out_shape=[jax.ShapeDtypeStruct(value.shape, F32) for value in grads]
        + [
            jax.ShapeDtypeStruct((half,) + parts.shape[1:], F32),
            jax.ShapeDtypeStruct((half,) + parts.shape[1:], BF16),
        ],
        compiler_params=params(),
        name="widen",
    )(*grads, parts)


def body(
    activations,
    cotangent,
    article_ids,
    section_proj,
    out_rows,
    up_rows,
    down_rows,
    norm_gains,
    slopes,
):
    section = lax.axis_index("section")
    core = section % 2
    first_chip = section < 2
    width = activations.shape[3]
    length = article_ids.shape[2]
    short = length // 3
    heads = 2 * slopes.shape[1]
    tile = length // 3

    (
        row, proj, out_weight, up_weight, down_weight, query, keyval, attended, middle, active,
        slant, grouped, long_rows, pooled, short_grad, gains, key_mark, short_query_mark,
        short_key_mark, keep,
    ) = first_call(
        activations, cotangent, article_ids, norm_gains, slopes, section_proj[0], out_rows,
        up_rows, down_rows, heads, tile,
    )
    exchanged = lax.ppermute(long_rows, "section", [(0, 2), (1, 3), (2, 0), (3, 1)])

    def zeros_of(call, *operands):
        return jax.tree.map(
            lambda leaf: jnp.zeros(leaf.shape, leaf.dtype), jax.eval_shape(call, *operands)
        )

    def short_all(pooled, grad):
        return short_call(
            pooled, grad, gains, short_query_mark, short_key_mark, proj, out_weight, up_weight,
            down_weight, heads,
        )

    short_result, pooled_grad, *short_grads = lax.cond(
        first_chip,
        lambda *operands: zeros_of(short_all, *operands),
        short_all,
        pooled,
        short_grad,
    )
    (proj_grad, out_grad, up_grad, down_grad, small), parts = last_call(
        row, gains, proj, key_mark, middle, attended, out_weight, keep, grouped, exchanged,
        active, slant, up_weight, down_weight, query, keyval,
        pooled_grad, short_result, *short_grads, tile=tile,
    )
    proj_grad, out_grad, up_grad, down_grad, input_grad, results = widen_call(
        (proj_grad, out_grad, up_grad, down_grad), parts
    )
    slope_grad = lax.dynamic_slice_in_dim(small[2], core * (heads // 2), heads // 2, 0)
    small = lax.dynamic_slice_in_dim(small, core, 1, 0)
    return (
        results[:, None],
        input_grad[:, None],
        proj_grad[None],
        out_grad,
        up_grad,
        down_grad,
        small,
        slope_grad.reshape(1, heads // 2),
    )


def solution(mesh):
    return jax.shard_map(
        body,
        mesh=mesh,
        in_specs=(
            P(None, "dp", "section", None),
            P(None, "dp", "section", None),
            P(None, "dp", None),
            P("section", None, None),
            P("section", None),
            P("section", None),
            P("section", None),
            P("section", None),
            P("section", None),
        ),
        out_specs=(
            P(None, "dp", "section", None),
            P(None, "dp", "section", None),
            P("section", None, None),
            P("section", None),
            P("section", None),
            P("section", None),
            P("section", None),
            P("section", None),
        ),
        check_vma=False,
    )
```

```python
import functools

import jax
import jax.numpy as jnp
from jax import lax
from jax.experimental import pallas as pl
from jax.experimental.pallas import tpu as pltpu
from jax.sharding import PartitionSpec as P

EPSILON = 1e-05
APART = -1e30
F32 = jnp.float32
BF16 = jnp.bfloat16
VMEM_LIMIT = 60 * 1024 * 1024
LANES = 128
PARTS = 4
HALF = 64
MESH = pl.DeviceIdType.MESH


def dot(left, right, left_dim, right_dim):
    return lax.dot_general(
        left, right, (((left_dim,), (right_dim,)), ((), ())), preferred_element_type=F32
    )


def standardize(value):
    centred = value - jnp.mean(value, axis=-1, keepdims=True)
    inverse = lax.rsqrt(jnp.mean(centred * centred, axis=-1, keepdims=True) + EPSILON)
    return centred * inverse, inverse


def norm_back(grad, gain, standard, inverse):
    scaled = grad * gain
    centred = (
        scaled
        - jnp.mean(scaled, axis=-1, keepdims=True)
        - standard * jnp.mean(scaled * standard, axis=-1, keepdims=True)
    )
    return centred * inverse


def params(limit=VMEM_LIMIT):
    return pltpu.CompilerParams(vmem_limit_bytes=limit)


def row_cuts(length, step):
    return [slice(start, start + step) for start in range(0, length, step)]


def lane_ids(rows):
    return lax.broadcasted_iota(jnp.int32, (rows, LANES), 1)


def barrier_with(devices):
    barrier = pltpu.get_barrier_semaphore()
    for device in devices:
        pl.semaphore_signal(barrier, inc=1, device_id=device, device_id_type=MESH)
    pl.semaphore_wait(barrier, len(devices))


def make_marks(wide, lane):
    length = wide.shape[0]
    mark = lane % HALF
    position = lax.broadcasted_iota(jnp.int32, (length, LANES), 0)
    low = position % 256
    same = wide == (mark - 2).astype(F32)
    chosen = (mark >= 2) & (mark < 5)
    query = jnp.where(chosen & same, 1.0, 0.0)
    fixed = jnp.where(mark < 8, 1.0, 0.0)
    apart = jnp.where(same, 0.0, APART)
    key = jnp.where(chosen, apart, fixed)
    key = jnp.where(mark == 0, low.astype(F32), key)
    key = jnp.where(mark == 1, (position - low).astype(F32), key)
    return query.astype(BF16), key.astype(BF16)


def gelu_pieces(value):
    root = 0.7978845608028654
    square = value * value
    inner = jnp.tanh(value * (root + (root * 0.044715) * square))
    half = 0.5 + 0.5 * inner
    active = value * half
    slant = half + active * (1.0 - inner) * (root + (3.0 * root * 0.044715) * square)
    return active, slant


LINE = 4
SQUARE = 2 * LINE


def head_back(
    side,
    key_mark_ref,
    query_ref,
    key_ref,
    value_ref,
    attended_ref,
    attended_grad_ref,
    mixed,
    keys,
    values,
    grads,
    key_sum,
    value_sum,
    cuts,
    tile,
):
    length = key_ref.shape[0]
    blocks = length // tile
    lane = lane_ids(tile)
    here = lane // HALF == side
    mark = lane % HALF
    earlier = lax.broadcasted_iota(jnp.int32, (tile, tile), 0) <= lax.broadcasted_iota(
        jnp.int32, (tile, tile), 1
    )
    position = lax.broadcasted_iota(jnp.int32, (tile, LANES), 0)
    spans = [slice(block * tile, (block + 1) * tile) for block in range(blocks)]
    for rows in spans:
        grad = attended_grad_ref[rows, :].astype(F32)
        product = jnp.where(here, grad * attended_ref[rows, :].astype(F32), 0.0)
        keys[rows, :] = jnp.where(
            here, key_ref[rows, :].astype(F32), key_mark_ref[rows, :].astype(F32)
        ).astype(BF16)
        values[rows, :] = jnp.where(here, value_ref[rows, :].astype(F32), 1.0).astype(BF16)
        centre = -jnp.sum(product, axis=1, keepdims=True)
        first = centre.astype(BF16).astype(F32)
        second = (centre - first).astype(BF16).astype(F32)
        third = centre - first - second
        marks = jnp.where(
            mark == 0, first, jnp.where(mark == 1, second, jnp.where(mark == 2, third, 0.0))
        )
        grads[rows, :] = jnp.where(here, grad, marks).astype(BF16)

    def score(block, other):
        rows, cols = spans[block], spans[other]
        raw = dot(keys[cols, :], query_ref[0, rows, :], 1, 1)
        return raw, dot(values[cols, :], grads[rows, :], 1, 1)

    def finish(block, other, raw, pull):
        rows, cols = spans[block], spans[other]
        weights = jnp.exp(raw)
        if other == block:
            weights = jnp.where(earlier, weights, 0.0)
        change = (weights * pull).astype(BF16)
        key_term = dot(change, query_ref[0, rows, :], 1, 0)
        value_term = dot(weights.astype(BF16), grads[rows, :], 1, 0)
        if other == block:
            key_sum[cols, :] = key_term
            value_sum[cols, :] = value_term
        else:
            key_sum[cols, :] += key_term
            value_sum[cols, :] += value_term
        return dot(change, keys[cols, :], 0, 0)

    def keep(rows, cut, value):
        mixed[rows, cut] = jnp.where(here, value, mixed[rows, cut].astype(F32)).astype(BF16)

    order = [(block, other) for block in range(blocks) for other in range(block + 1)]
    ahead = score(*order[0])
    slope_sum = jnp.zeros((tile, LANES), F32)
    total = None
    for index, (block, other) in enumerate(order):
        now = ahead
        if index + 1 < len(order):
            ahead = score(*order[index + 1])
        term = finish(block, other, *now)
        total = term if other == 0 else total + term
        if other == block:
            place = -(position + block * tile).astype(F32)
            slope_sum = slope_sum + jnp.where(
                mark < 2, total, jnp.where(mark == 5, total * place, 0.0)
            )
            keep(spans[block], cuts[0], total * 0.125)
    for rows in spans:
        keep(rows, cuts[1], key_sum[rows, :])
        keep(rows, cuts[2], value_sum[rows, :])
    return jnp.sum(jnp.where(here, 0.0, slope_sum))


def head_cuts(pair, width):
    return [
        pl.ds(pl.multiple_of(place * width + pair * LANES, LANES), LANES) for place in range(3)
    ]


def first_kernel(
    act_ref,
    cot_ref,
    ids_ref,
    gain_ref,
    slope_ref,
    proj_src,
    out_src,
    up_src,
    down_src,
    row_dst,
    proj_dst,
    out_dst,
    up_dst,
    down_dst,
    query_dst,
    keyval_dst,
    attended_dst,
    middle_dst,
    active_dst,
    slant_dst,
    grouped_dst,
    long_dst,
    pooled_dst,
    back_dst,
    added_dst,
    small_all,
    key_mark,
    short_query_mark,
    short_key_mark,
    keep_ref,
    row_ref,
    proj_all,
    out_all,
    up_all,
    down_all,
    query_mark,
    wide_ref,
    mixed,
    queries,
    keys,
    values,
    attended,
    middle,
    actives,
    slants,
    moved,
    grouped,
    result,
    pooled_own,
    pooled,
    back,
    added,
    load_sem,
    row_send,
    row_recv,
    pair_send,
    pair_recv,
    pool_send,
    pool_recv,
    done_sem,
    cot_send,
    cot_recv,
    *,
    tile,
    heads,
):
    section = lax.axis_index("section")
    group = lax.axis_index("dp")
    sections = 4
    core = section % 2
    chip = section // 2
    partner = chip * 2 + (1 - core)
    quarter, width = act_ref.shape[2:]
    length = row_ref.shape[0]
    short = length // 3
    groups = width // LANES
    units = up_all.shape[1]
    piece = units // PARTS
    blocks = length // tile

    def span_of(whole):
        rows = whole.shape[0] // 2
        return pl.ds(pl.multiple_of(core * rows, rows), rows)

    wholes = (proj_all, small_all, out_all, up_all, down_all)
    shards = (proj_src, None, out_src, up_src, down_src)

    def load_copy(index):
        return pltpu.make_async_copy(
            shards[index], wholes[index].at[span_of(wholes[index]), :], load_sem.at[index]
        )

    for index in (0, 2, 3, 4):
        load_copy(index).start()
    small_rows = span_of(small_all)
    small_all[small_rows, :] = jnp.concatenate(
        [
            gain_ref[...].astype(F32),
            jnp.concatenate(
                [
                    slope_ref[...].astype(F32),
                    jnp.zeros((1, width - slope_ref.shape[1]), F32),
                ],
                axis=1,
            ),
            jnp.zeros((6, width), F32),
        ],
        axis=0,
    )
    others = [lax.rem(section + hop, sections) for hop in range(1, sections)]
    barrier_with([(other, group) for other in others])
    place = pl.ds(pl.multiple_of(section * quarter, quarter), quarter)

    def row_copy(source_ref, hop):
        target = lax.rem(section + hop, sections)
        return pltpu.make_async_remote_copy(
            src_ref=source_ref.at[target % 2, 0],
            dst_ref=row_ref.at[place, :],
            send_sem=row_send.at[hop],
            recv_sem=row_recv.at[hop],
            device_id=(target, group),
            device_id_type=MESH,
        )

    for hop in (2, 1, 3):
        target_chip = lax.rem(section + hop, sections) // 2

        @pl.when(target_chip == 0)
        def _():
            row_copy(act_ref, hop).start()

        @pl.when(target_chip == 1)
        def _():
            row_copy(cot_ref, hop).start()

    def pair_copy(index):
        spot = wholes[index].at[span_of(wholes[index]), :]
        return pltpu.make_async_remote_copy(
            src_ref=spot,
            dst_ref=spot,
            send_sem=pair_send.at[index],
            recv_sem=pair_recv.at[index],
            device_id=(partner, group),
            device_id_type=MESH,
        )

    for index in range(len(wholes)):
        if shards[index] is not None:
            load_copy(index).wait()
        pair_copy(index).start()

    @pl.when(chip == 0)
    def _():
        row_ref[place, :] = act_ref[core, 0]

    @pl.when(chip == 1)
    def _():
        row_ref[place, :] = cot_ref[core, 0]

    ids = jnp.broadcast_to(ids_ref[core].astype(F32), (LANES, length))
    wide = ids.T
    wide_ref[0:8, :] = jnp.full((8, LANES), -1.0, F32)
    wide_ref[8:, :] = wide
    query_mark[...], key_mark[...] = make_marks(wide, lane_ids(length))
    short_wide = wide_ref[pl.ds(8, short, stride=3), :]
    short_query_mark[...], short_key_mark[...] = make_marks(short_wide, lane_ids(short))
    for turn in range(3):
        current = wide_ref[pl.ds(8 + turn, short, stride=3), :]
        before = wide_ref[pl.ds(6 + turn, short, stride=3), :]
        keep_ref[turn] = jnp.where(current == before, 1.0, 0.0)
    pair_copy(0).wait_recv()
    pair_copy(1).wait_recv()

    @pl.when(core == 0)
    def _():
        row_copy(act_ref, 3).wait_recv()

    @pl.when(core == 1)
    def _():
        row_copy(act_ref, 1).wait_recv()

    lane = lane_ids(tile)
    upper = lane >= HALF
    mark = lane % HALF
    sides = (jnp.logical_not(upper), upper)
    earlier = lax.broadcasted_iota(jnp.int32, (tile, tile), 0) >= lax.broadcasted_iota(
        jnp.int32, (tile, tile), 1
    )
    spans = [slice(block * tile, (block + 1) * tile) for block in range(blocks)]

    def project(rows):
        standard, _ = standardize(row_ref[rows, :].astype(F32))
        normal = (standard * small_all[0:1, :]).astype(BF16)
        mixed[rows, :] = dot(normal, proj_all[0:width, :], 1, 0).astype(BF16)

    def attend(members):
        def attend_pair(pair, carry):
            cuts = head_cuts(pair, width)
            column = lax.broadcasted_iota(jnp.int32, (1, width), 1)
            per = heads // 2
            slope_of = []
            for side in range(2):
                number = 2 * pair + side
                slopes = jnp.where(number < per, small_all[1:2, :], small_all[9:10, :])
                slope_of.append(
                    jnp.sum(
                        jnp.where(column == number % per, slopes, 0.0), axis=1, keepdims=True
                    )
                )
            for block in members:
                rows = spans[block]
                key_rows = mixed[rows, cuts[1]].astype(F32)
                value_rows = mixed[rows, cuts[2]].astype(F32)
                marks = key_mark[rows, :].astype(F32)
                for side, here in enumerate(sides):
                    keys[2 * pair + side, rows, :] = jnp.where(here, key_rows, marks).astype(BF16)
                    values[2 * pair + side, rows, :] = jnp.where(here, value_rows, 1.0).astype(
                        BF16
                    )

            def score(block, side):
                rows = spans[block]
                marks = jnp.where(mark < 2, slope_of[side], query_mark[rows, :].astype(F32))
                query = jnp.where(sides[side], mixed[rows, cuts[0]].astype(F32) * 0.125, marks)
                query = query.astype(BF16)
                number = 2 * pair + side
                near = jnp.where(earlier, dot(query, keys[number, rows, :], 1, 1), APART)
                far = dot(query, keys[number, : block * tile, :], 1, 1) if block else None
                return query, near, far

            def finish(block, side, query, near, far):
                rows = spans[block]
                number = 2 * pair + side
                highest = jnp.max(near, axis=1, keepdims=True)
                if block:
                    highest = jnp.maximum(highest, jnp.max(far, axis=1, keepdims=True))
                mass = dot(jnp.exp(near - highest).astype(BF16), values[number, rows, :], 1, 0)
                if block:
                    mass = mass + dot(
                        jnp.exp(far - highest).astype(BF16),
                        values[number, : block * tile, :],
                        1,
                        0,
                    )
                level = -(highest + jnp.log(mass))
                first = level.astype(BF16).astype(F32)
                second = (level - first).astype(BF16).astype(F32)
                third = level - first - second
                query = query.astype(F32)
                level_marks = jnp.where(
                    mark == 5,
                    first,
                    jnp.where(mark == 6, second, jnp.where(mark == 7, third, query)),
                )
                queries[number, rows, :] = jnp.where(sides[side], query, level_marks).astype(BF16)
                return mass / pltpu.roll(mass, HALF, 1)

            order = [(block, side) for block in members for side in range(2)]
            ahead = score(*order[0])
            shares = [None, None]
            for index, (block, side) in enumerate(order):
                now = ahead
                if index + 1 < len(order):
                    ahead = score(*order[index + 1])
                shares[side] = finish(block, side, *now)
                if side:
                    attended[spans[block], cuts[0]] = jnp.where(
                        upper, shares[1], shares[0]
                    ).astype(BF16)
            return carry

        lax.fori_loop(0, heads // 2, attend_pair, 0)

    def rows_wait_rest():
        row_copy(act_ref, 2).wait_recv()

        @pl.when(core == 0)
        def _():
            row_copy(act_ref, 1).wait_recv()

        @pl.when(core == 1)
        def _():
            row_copy(act_ref, 3).wait_recv()

    def pool_copy(block):
        rows = pl.ds(block * (tile // 3), tile // 3)
        return pltpu.make_async_remote_copy(
            src_ref=pooled_own.at[rows, :],
            dst_ref=pooled.at[rows, :],
            send_sem=pool_send.at[block],
            recv_sem=pool_recv.at[block],
            device_id=(lax.rem(section + 2, sections), group),
            device_id_type=MESH,
        )

    def out_copies(members=range(6)):
        kept = [
            (proj_all, proj_dst),
            (out_all, out_dst),
            (up_all, up_dst),
            (down_all, down_dst),
            (row_ref, row_dst),
            (grouped, grouped_dst),
        ]
        return [
            pltpu.make_async_copy(*kept[member], done_sem.at[member]) for member in members
        ]

    def attend_copies():
        kept = [
            (queries, query_dst),
            (mixed.at[:, pl.ds(width, 2 * width)], keyval_dst),
            (attended, attended_dst),
        ]
        return [
            pltpu.make_async_copy(origin, target, done_sem.at[6 + index])
            for index, (origin, target) in enumerate(kept)
        ]

    def tile_copies(block):
        rows = pl.ds(block * tile, tile)
        kept = [(middle, middle_dst), (actives, active_dst), (slants, slant_dst), (result, long_dst)]
        return [
            pltpu.make_async_copy(
                origin.at[rows, :], target.at[rows, :], done_sem.at[9 + 4 * block + index]
            )
            for index, (origin, target) in enumerate(kept)
        ]

    def dense_tile(block):
        rows = spans[block]
        value = row_ref[rows, :].astype(F32) + dot(attended[rows, :], out_all[...], 1, 0)
        middle[rows, :] = value
        standard, _ = standardize(value)
        normal = (standard * small_all[8:9, :]).astype(BF16)
        for part in range(PARTS):
            span = slice(part * piece, (part + 1) * piece)
            active, slant = gelu_pieces(dot(normal, up_all[:, span], 1, 0))
            active = active.astype(BF16)
            actives[rows, span] = active
            slants[rows, span] = slant.astype(BF16)
            value = value + dot(active, down_all[span, :], 1, 0)
        low = value.astype(BF16)
        result[rows, :] = low
        for copy in tile_copies(block):
            copy.start()
        small_tile = tile // 3
        for part in range(groups):
            lanes = slice(part * LANES, (part + 1) * LANES)
            moved[part, 8 + block * tile : 8 + (block + 1) * tile, :] = low[:, lanes].astype(
                F32
            )
        total = None
        small_rows = slice(block * small_tile, (block + 1) * small_tile)
        for turn in range(3):
            picked = jnp.concatenate(
                [
                    moved[part, pl.ds(6 + turn + block * tile, small_tile, stride=3), :]
                    for part in range(groups)
                ],
                axis=1,
            )
            factor = jnp.concatenate([keep_ref[turn, small_rows, :]] * groups, axis=1)
            picked = (picked * factor).astype(BF16)
            cut = slice(turn * width, (turn + 1) * width)
            grouped[small_rows, cut] = picked
            term = dot(picked, proj_all[width : 2 * width, cut], 1, 1)
            total = term if total is None else total + term
        pooled_own[small_rows, :] = total.astype(BF16)
        pool_copy(block).start()

    def cot_copy():
        return pltpu.make_async_remote_copy(
            src_ref=row_ref,
            dst_ref=added,
            send_sem=cot_send.at[0],
            recv_sem=cot_recv.at[0],
            device_id=(lax.rem(section + 2, sections), group),
            device_id_type=MESH,
        )

    @pl.when(chip == 0)
    def _():
        for start in range(0, 2 * quarter, quarter):
            project(slice(start, start + quarter))
        attend((0,))
        for part in range(groups):
            moved[part, 0:8, :] = jnp.zeros((8, LANES), F32)

    for index in range(2, len(wholes)):
        pair_copy(index).wait_recv()

    @pl.when(chip == 0)
    def _():
        dense_tile(0)

    rows_wait_rest()

    @pl.when(chip == 1)
    def _():
        cot_copy().start()

    for copy in out_copies(range(5)):
        copy.start()

    @pl.when(chip == 0)
    def _():
        for start in range(2 * quarter, length, quarter):
            project(slice(start, start + quarter))
        attend(tuple(range(1, blocks)))
        for copy in attend_copies():
            copy.start()
        for block in range(1, blocks):
            dense_tile(block)

    @pl.when(chip == 1)
    def _():
        for part in range(groups):
            lanes = slice(part * LANES, (part + 1) * LANES)
            moved[part, 8:, :] = row_ref[:, lanes].astype(F32)
        for turn in range(3):
            for part in range(groups):
                left = turn * width + part * LANES
                grouped[:, left : left + LANES] = moved[
                    part, pl.ds(8 + turn, short, stride=3), :
                ].astype(BF16)
        back[...] = dot(grouped[...], proj_all[width : 2 * width, :], 1, 1).astype(BF16)
        back_copy = pltpu.make_async_copy(back, back_dst, done_sem.at[21])
        back_copy.start()
        back_copy.wait()
        for block in range(blocks):
            pool_copy(block).wait_recv()
        pooled_copy = pltpu.make_async_copy(pooled, pooled_dst, done_sem.at[23])
        pooled_copy.start()
        pooled_copy.wait()
        cot_copy().wait_send()

    out_copies([5])[0].start()

    @pl.when(chip == 0)
    def _():
        for copy in attend_copies():
            copy.wait()
        for block in range(blocks):
            for copy in tile_copies(block):
                copy.wait()
            pool_copy(block).wait_send()
        cot_copy().wait_recv()
        added_copy = pltpu.make_async_copy(added, added_dst, done_sem.at[22])
        added_copy.start()
        added_copy.wait()

    for copy in out_copies():
        copy.wait()
    for index in range(len(wholes)):
        pair_copy(index).wait_send()
    for hop in range(1, sections):
        row_copy(act_ref, hop).wait_send()


def first_call(
    activations, cotangent, ids, gains, slopes, proj, out_rows, up_rows, down_rows, heads, tile
):
    inside = pl.BlockSpec(memory_space=pltpu.VMEM)
    anywhere = pl.BlockSpec(memory_space=pl.ANY)
    quarter, width = activations.shape[2:]
    length = 4 * quarter
    short = length // 3
    units = up_rows.shape[1]
    shape = jax.ShapeDtypeStruct
    vmem = pltpu.VMEM
    twice = lambda value: (2 * value.shape[0], value.shape[1])
    weights = [twice(value) for value in (proj, out_rows, up_rows, down_rows)]
    return pl.pallas_call(
        functools.partial(first_kernel, tile=tile, heads=heads),
        in_specs=[inside] * 5 + [anywhere] * 4,
        out_specs=[anywhere] * 16 + [inside] * 5,
        out_shape=[shape((length, width), BF16)]
        + [shape(size, BF16) for size in weights]
        + [
            shape((heads, length, LANES), BF16),
            shape((length, 2 * width), BF16),
            shape((length, width), BF16),
            shape((length, width), F32),
            shape((length, units), BF16),
            shape((length, units), BF16),
            shape((short, 3 * width), BF16),
            shape((length, width), BF16),
            shape((short, width), BF16),
            shape((short, width), BF16),
            shape((length, width), BF16),
            shape((16, width), F32),
            shape((length, LANES), BF16),
            shape((short, LANES), BF16),
            shape((short, LANES), BF16),
            shape((3, short, LANES), F32),
        ],
        scratch_shapes=[vmem((length, width), BF16)]
        + [vmem(size, BF16) for size in weights]
        + [
            vmem((length, LANES), BF16),
            vmem((length + 8, LANES), F32),
            vmem((length, 3 * width), BF16),
            vmem((heads, length, LANES), BF16),
            vmem((heads, length, LANES), BF16),
            vmem((heads, length, LANES), BF16),
            vmem((length, width), BF16),
            vmem((length, width), F32),
            vmem((length, units), BF16),
            vmem((length, units), BF16),
            vmem((width // LANES, length + 8, LANES), F32),
            vmem((short, 3 * width), BF16),
            vmem((length, width), BF16),
            vmem((short, width), BF16),
            vmem((short, width), BF16),
            vmem((short, width), BF16),
            vmem((length, width), BF16),
            pltpu.SemaphoreType.DMA((5,)),
            pltpu.SemaphoreType.DMA((4,)),
            pltpu.SemaphoreType.DMA((4,)),
            pltpu.SemaphoreType.DMA((5,)),
            pltpu.SemaphoreType.DMA((5,)),
            pltpu.SemaphoreType.DMA((3,)),
            pltpu.SemaphoreType.DMA((3,)),
            pltpu.SemaphoreType.DMA((24,)),
            pltpu.SemaphoreType.DMA((1,)),
            pltpu.SemaphoreType.DMA((1,)),
        ],
        compiler_params=pltpu.CompilerParams(
            collective_id=0, has_side_effects=True, vmem_limit_bytes=VMEM_LIMIT
        ),
        name="first",
    )(activations, cotangent, ids, gains, slopes, proj, out_rows, up_rows, down_rows)


def short_kernel(
    hidden_ref,
    grad_ref,
    gain_ref,
    query_mark_ref,
    key_mark_ref,
    proj_src,
    out_src,
    up_src,
    down_src,
    result_dst,
    hidden_dst,
    even_dst,
    out_dst,
    up_dst,
    down_dst,
    small_ref,
    proj_ref,
    out_ref,
    up_ref,
    down_ref,
    result_ref,
    hidden_grad,
    even_grad,
    out_grad,
    up_grad,
    down_grad,
    mixed,
    queries,
    keys,
    values,
    grads,
    key_sum,
    value_sum,
    attended,
    middle,
    total,
    normal,
    flip,
    grad_flip,
    actives,
    slants,
    attended_grad,
    mixed_grad,
    load_sem,
    done_sem,
    *,
    heads,
):
    length, width = hidden_ref.shape
    units = up_ref.shape[1]
    piece = units // PARTS
    loads = [
        pltpu.make_async_copy(origin, target, load_sem.at[index])
        for index, (origin, target) in enumerate(
            (
                (proj_src.at[0:width, :], proj_ref),
                (out_src, out_ref),
                (up_src, up_ref),
                (down_src, down_ref),
            )
        )
    ]
    for copy in loads:
        copy.start()
    lane = lane_ids(length)
    upper = lane >= HALF
    mark = lane % HALF
    earlier = lax.broadcasted_iota(jnp.int32, (length, length), 0) >= lax.broadcasted_iota(
        jnp.int32, (length, length), 1
    )
    standard, _ = standardize(hidden_ref[...].astype(F32))
    low = (standard * gain_ref[0:1, :]).astype(BF16)
    flip[...] = low.T
    loads[0].wait()
    mixed[...] = dot(low, proj_ref[...], 1, 0).astype(BF16)
    small_ref[...] = jnp.zeros_like(small_ref)
    column = lax.broadcasted_iota(jnp.int32, (1, width), 1)
    sides = (jnp.logical_not(upper), upper)
    per = heads // 2

    def attend_pair(pair, carry):
        cuts = head_cuts(pair, width)
        query_rows = mixed[:, cuts[0]].astype(F32) * 0.125
        key_rows = mixed[:, cuts[1]].astype(F32)
        value_rows = mixed[:, cuts[2]].astype(F32)
        scores, parts = [], []
        for side, here in enumerate(sides):
            number = 2 * pair + side
            slopes = jnp.where(number < per, gain_ref[1:2, :], gain_ref[9:10, :])
            slope = jnp.sum(jnp.where(column == number % per, slopes, 0.0), axis=1, keepdims=True)
            keys[side] = jnp.where(here, key_rows, key_mark_ref[...].astype(F32)).astype(BF16)
            values[side] = jnp.where(here, value_rows, 1.0).astype(BF16)
            marks = jnp.where(mark < 2, slope, query_mark_ref[...].astype(F32))
            query = jnp.where(here, query_rows, marks).astype(BF16)
            parts.append(query)
            scores.append(jnp.where(earlier, dot(query, keys[side], 1, 1), APART))
        shares = []
        for side, here in enumerate(sides):
            highest = jnp.max(scores[side], axis=1, keepdims=True)
            mass = dot(jnp.exp(scores[side] - highest).astype(BF16), values[side], 1, 0)
            level = -(highest + jnp.log(mass))
            first = level.astype(BF16).astype(F32)
            second = (level - first).astype(BF16).astype(F32)
            third = level - first - second
            query = parts[side].astype(F32)
            level_marks = jnp.where(
                mark == 5, first, jnp.where(mark == 6, second, jnp.where(mark == 7, third, query))
            )
            queries[2 * pair + side] = jnp.where(here, query, level_marks).astype(BF16)
            shares.append(mass / pltpu.roll(mass, HALF, 1))
        attended[:, cuts[0]] = jnp.where(upper, shares[1], shares[0]).astype(BF16)
        return carry

    lax.fori_loop(0, heads // 2, attend_pair, 0)
    loads[1].wait()
    value = hidden_ref[...].astype(F32) + dot(attended[...], out_ref[...], 1, 0)
    middle[...] = value
    total[...] = value
    standard, _ = standardize(value)
    normal[...] = (standard * gain_ref[8:9, :]).astype(BF16)
    loads[2].wait()
    loads[3].wait()
    for part in range(PARTS):
        span = slice(part * piece, (part + 1) * piece)
        raised = dot(normal[...], up_ref[:, span], 1, 0)
        active, slant = gelu_pieces(raised)
        active = active.astype(BF16)
        actives[:, span] = active
        slants[:, span] = slant.astype(BF16)
        total[...] += dot(active, down_ref[span, :], 1, 0)
    result_ref[...] = total[...].astype(BF16)
    results = [pltpu.make_async_copy(result_ref, result_dst, done_sem.at[0])]
    results[0].start()

    grad_flip[...] = grad_ref[...].T
    normal_flip = normal[...].T
    for part in range(PARTS):
        span = slice(part * piece, (part + 1) * piece)
        down_grad[span, :] = dot(grad_flip[...], actives[:, span], 1, 0).astype(BF16).T
        grad_active = dot(grad_ref[...], down_ref[span, :], 1, 1)
        low = (grad_active * slants[:, span].astype(F32)).astype(BF16)
        term = dot(low, up_ref[:, span], 1, 1)
        if part:
            total[...] += term
        else:
            total[...] = term
        up_grad[:, span] = dot(normal_flip, low, 1, 0).astype(BF16)
    for index, (origin, target) in enumerate(((down_grad, down_dst), (up_grad, up_dst))):
        results.append(pltpu.make_async_copy(origin, target, done_sem.at[1 + index]))
        results[-1].start()
    standard, inverse = standardize(middle[...])
    grad = total[...]
    small_ref[1:2, :] = jnp.sum(grad * standard, axis=0, keepdims=True)
    middle_grad = grad_ref[...].astype(F32) + norm_back(grad, gain_ref[8:9, :], standard, inverse)
    total[...] = middle_grad
    low = middle_grad.astype(BF16)
    attended_grad[...] = dot(low, out_ref[...], 1, 1).astype(BF16)
    out_grad[...] = dot(attended[...], low, 0, 0).astype(BF16)
    results.append(pltpu.make_async_copy(out_grad, out_dst, done_sem.at[3]))
    results[-1].start()

    def back_pair(pair, carry):
        cuts = head_cuts(pair, width)
        for side in range(2):
            slope_grad = head_back(
                side, key_mark_ref, queries.at[pl.ds(2 * pair + side, 1)], mixed.at[:, cuts[1]],
                mixed.at[:, cuts[2]], attended.at[:, cuts[0]], attended_grad.at[:, cuts[0]],
                mixed_grad, keys.at[side], values.at[side], grads.at[side], key_sum.at[side],
                value_sum.at[side], cuts, length,
            )
            small_ref[2:3, :] += jnp.where(column == 2 * pair + side, slope_grad, 0.0)
        return carry

    lax.fori_loop(0, heads // 2, back_pair, 0)
    for place in range(3):
        span = slice(place * width, (place + 1) * width)
        even_grad[:, span] = dot(flip[...], mixed_grad[:, span], 1, 0).astype(BF16)
    results.append(pltpu.make_async_copy(even_grad, even_dst, done_sem.at[4]))
    results[-1].start()
    standard, inverse = standardize(hidden_ref[...].astype(F32))
    grad = dot(mixed_grad[...], proj_ref[...], 1, 1)
    small_ref[0:1, :] = jnp.sum(grad * standard, axis=0, keepdims=True)
    hidden_grad[...] = (
        total[...] + norm_back(grad, gain_ref[0:1, :], standard, inverse)
    ).astype(BF16)
    results.append(pltpu.make_async_copy(hidden_grad, hidden_dst, done_sem.at[5]))
    results[-1].start()
    for copy in results:
        copy.wait()


def short_call(
    hidden, grad, gains, query_mark, key_mark, proj, out_weight, up_weight, down_weight, heads
):
    inside = pl.BlockSpec(memory_space=pltpu.VMEM)
    anywhere = pl.BlockSpec(memory_space=pl.ANY)
    length, width = hidden.shape
    units = up_weight.shape[1]
    vmem = pltpu.VMEM
    shape = jax.ShapeDtypeStruct
    grads = [(width, 3 * width), out_weight.shape, up_weight.shape, down_weight.shape]
    return pl.pallas_call(
        functools.partial(short_kernel, heads=heads),
        in_specs=[inside] * 5 + [anywhere] * 4,
        out_specs=[anywhere] * 6 + [inside],
        out_shape=[shape((length, width), BF16)] * 2
        + [shape(size, BF16) for size in grads]
        + [shape((8, width), F32)],
        scratch_shapes=[
            vmem((width, 3 * width), BF16),
            vmem(out_weight.shape, BF16),
            vmem(up_weight.shape, BF16),
            vmem(down_weight.shape, BF16),
            vmem((length, width), BF16),
            vmem((length, width), BF16),
        ]
        + [vmem(size, BF16) for size in grads]
        + [
            vmem((length, 3 * width), BF16),
            vmem((heads, length, LANES), BF16),
            vmem((2, length, LANES), BF16),
            vmem((2, length, LANES), BF16),
            vmem((2, length, LANES), BF16),
            vmem((2, length, LANES), F32),
            vmem((2, length, LANES), F32),
            vmem((length, width), BF16),
            vmem((length, width), F32),
            vmem((length, width), F32),
            vmem((length, width), BF16),
            vmem((width, length), BF16),
            vmem((width, length), BF16),
            vmem((length, units), BF16),
            vmem((length, units), BF16),
            vmem((length, width), BF16),
            vmem((length, 3 * width), BF16),
            pltpu.SemaphoreType.DMA((4,)),
            pltpu.SemaphoreType.DMA((6,)),
        ],
        compiler_params=params(),
        name="short",
    )(hidden, grad, gains, query_mark, key_mark, proj, out_weight, up_weight, down_weight)


def chunk_list():
    chunks = [("odd", 1, 0, 512, place * 512, 512) for place in range(3)]
    chunks += [("up", None, 0, 256, place * 512, 512) for place in (0, 2)]
    chunks += [("down", None, 0, 512, 0, 512)]
    chunks += [("up", None, 0, 256, place * 512, 512) for place in (1, 3)]
    chunks += [("down", None, 512, 512, 0, 512)]
    chunks += [("out", None, 0, 256, 0, 512)]
    chunks += [("even", 0, 0, 512, pair * 384, 384) for pair in range(4)]
    return chunks


BEGINS = {1: (3,), 2: (4, 5), 3: (6,), 4: (7, 8, 9), 6: (10,), 8: (11,), 10: (12,), 12: (13,)}
TICKS = {
    3: [
        ("pair", 3), ("side", 1), ("side", 2), ("line", 0),
    ],
    4: [
        ("pair", 5), ("side", 3), ("line", 1), ("line", 2), ("side", 4),
    ],
    5: [
        ("line", 3), ("side", 5),
    ],
    6: [
        ("back", 1), ("side", 6), ("pair", 7), ("pair", 9), ("back", 2), ("pair", 8),
        ("full", 0), ("line", 4),
    ],
    7: [
        ("full", 1), ("back", 3), ("side", 7),
    ],
    8: [
        ("pair", 10), ("side", 9), ("line", 5), ("full", 2), ("line", 6),
    ],
    9: [
        ("back", 4), ("side", 8),
    ],
    10: [
        ("line", 7), ("pair", 11), ("full", 3), ("line", 9), ("side", 10),
    ],
    11: [
        ("full", 4), ("back", 5), ("side", 11),
    ],
    12: [
        ("back", 6), ("pair", 12),
    ],
    13: [
        ("line", 8), ("full", 5),
    ],
}
MIDDLES = {
    1: [
        ("pair", 0), ("pair", 1), ("pair", 2),
    ],
    2: [
        ("side", 0),
    ],
    3: [
        ("pair", 4),
    ],
    4: [
        ("pair", 6), ("back", 0),
    ],
}
DRAIN = [
    ("full", 6), ("back", 7), ("pair", 13), ("side", 12), ("back", 9), ("line", 10),
    ("line", 11), ("full", 7), ("side", 13), ("back", 8), ("full", 9), ("line", 12),
    ("back", 10), ("back", 11), ("full", 8), ("line", 13), ("full", 10), ("back", 12),
    ("full", 11), ("back", 13), ("full", 12), ("full", 13),
]


def last_kernel(
    hidden_src,
    gain_ref,
    proj_src,
    key_mark_src,
    middle_src,
    attended_src,
    out_weight_src,
    keep_src,
    grouped_src,
    added_src,
    active_ref,
    slant_ref,
    up_weight_ref,
    down_weight_ref,
    query_ref,
    key_ref,
    value_ref,
    long_src,
    pooled_grad_ref,
    short_result_ref,
    even_ref,
    out_ref,
    up_ref,
    down_ref,
    small_ref,
    proj_result,
    out_result,
    up_result,
    down_result,
    small_result,
    parts_result,
    middle_ref,
    attended_ref,
    out_weight_ref,
    hidden_ref,
    key_mark_ref,
    proj_ref,
    keep_ref,
    grouped_ref,
    added_ref,
    sent_long,
    short_rows,
    sent_rows,
    moved,
    rows_buf,
    normal,
    grad_flip,
    total,
    lower,
    attended_grad,
    mixed,
    keys,
    values,
    grads,
    key_sum,
    value_sum,
    even_grad,
    odd_grad,
    out_grad,
    up_grad,
    down_grad,
    small_grad,
    small_full,
    parts_ref,
    proj_full,
    out_full,
    up_full,
    down_full,
    proj_pair,
    out_pair,
    up_pair,
    down_pair,
    proj_side,
    out_side,
    up_side,
    down_side,
    proj_line,
    out_line,
    up_line,
    down_line,
    small_pair,
    small_side,
    small_line,
    local_sem,
    pair_send,
    pair_recv,
    side_send,
    side_recv,
    line_send,
    line_recv,
    back_send,
    back_recv,
    full_send,
    full_recv,
    small_send,
    small_recv,
    rows_send,
    rows_recv,
    result_sem,
    load_sem,
    short_send,
    short_recv,
    early_sem,
    *,
    tile,
):
    step = pl.program_id(0)
    last = pl.num_programs(0) - 1
    section = lax.axis_index("section")
    group = lax.axis_index("dp")
    core = section % 2
    chip = section // 2
    partner = (chip * 2 + (1 - core), group)
    base = group // SQUARE * SQUARE
    side = group % 2
    line = group % SQUARE // 2
    neighbour = (section, base + line * 2 + (1 - side))
    length, width = hidden_ref.shape
    short = length // 3
    groups = width // LANES
    stride = min(length // 2, 384)
    quarter = parts_ref.shape[1]
    chunks = chunk_list()
    first_head = 1 + PARTS

    def along(hop):
        return (section, base + lax.rem(line + hop, LINE) * 2 + side)

    def across(hop):
        return lax.rem(section + hop, 4)

    source = {"odd": odd_grad, "even": even_grad, "out": out_grad, "up": up_grad, "down": down_grad}
    table = lambda proj, out, up, down: {
        "odd": proj, "even": proj, "out": out, "up": up, "down": down
    }
    sums = table(proj_pair, out_pair, up_pair, down_pair)
    sides = table(proj_side, out_side, up_side, down_side)
    lines = table(proj_line, out_line, up_line, down_line)
    fulls = table(proj_full, out_full, up_full, down_full)
    outcomes = table(proj_result, out_result, up_result, down_result)

    def cut(start, size):
        return pl.ds(pl.multiple_of(start, 16), size)

    def remote(origin, target, send, recv, device):
        return pltpu.make_async_remote_copy(
            src_ref=origin,
            dst_ref=target,
            send_sem=send,
            recv_sem=recv,
            device_id=device,
            device_id_type=MESH,
        )

    def pair_copy(index):
        name, owner, start, rows, left, cols = chunks[index]
        offset = 0 if owner is not None else (1 - core) * (source[name].shape[0] // 2)
        lanes = pl.ds(left, cols)
        return remote(
            source[name].at[cut(offset + start, rows), lanes],
            sums[name].at[cut(start, rows), lanes],
            pair_send.at[index],
            pair_recv.at[index],
            partner,
        )

    def side_copy(index):
        name, _, start, rows, left, cols = chunks[index]
        half = rows // 2
        lanes = pl.ds(left, cols)
        return remote(
            sums[name].at[cut(start + (1 - side) * half, half), lanes],
            sides[name].at[cut(start // 2, half), lanes],
            side_send.at[index],
            side_recv.at[index],
            neighbour,
        )

    def line_copy(index, hop):
        name, _, start, rows, left, cols = chunks[index]
        half, piece = rows // 2, rows // SQUARE
        lanes = pl.ds(left, cols)
        target = lax.rem(line + hop, LINE)
        return remote(
            sums[name].at[cut(start + side * half + target * piece, piece), lanes],
            lines[name].at[hop - 1, cut(start // SQUARE, piece), lanes],
            line_send.at[index, hop - 1],
            line_recv.at[index, hop - 1],
            along(hop),
        )

    def back_copy(index, hop):
        name, _, start, rows, left, cols = chunks[index]
        half, piece = rows // 2, rows // SQUARE
        place = fulls[name].at[
            cut(start + side * half + line * piece, piece), pl.ds(left, cols)
        ]
        return remote(
            place, place, back_send.at[index, hop - 1], back_recv.at[index, hop - 1], along(hop)
        )

    def full_copy(index):
        name, _, start, rows, left, cols = chunks[index]
        half = rows // 2
        place = fulls[name].at[cut(start + side * half, half), pl.ds(left, cols)]
        return remote(place, place, full_send.at[index], full_recv.at[index], neighbour)

    def result_copies(index):
        name, _, start, rows, left, cols = chunks[index]
        spans = [(pl.ds(left, cols), pl.ds(left, cols))]
        if name == "even":
            spans = [span for span in regroup() if left <= span[1].start < left + cols]
        return [
            pltpu.make_async_copy(
                fulls[name].at[cut(start, rows), held],
                outcomes[name].at[cut(start, rows), final],
                result_sem.at[index, number],
            )
            for number, (final, held) in enumerate(spans)
        ]

    def owned(index, act):
        owner = chunks[index][1]
        if owner is None:
            act()
        else:
            pl.when(core == owner)(act)

    def pair_start(index):
        owner = chunks[index][1]
        begin = lambda: pair_copy(index).start()
        if owner is None:
            begin()
        else:
            pl.when(core != owner)(begin)

    def pair_stage(index):
        name, owner, start, rows, left, cols = chunks[index]
        lanes = slice(left, left + cols)
        here = cut(start, rows)

        def act():
            pair_copy(index).wait_recv()
            offset = 0 if owner is not None else core * (source[name].shape[0] // 2)
            mine = source[name][cut(offset + start, rows), lanes].astype(F32)
            arrived = sums[name][here, lanes].astype(F32)
            sums[name][here, lanes] = (mine + arrived).astype(BF16)
            side_copy(index).start()

        if owner is None:
            pair_copy(index).wait_send()
        else:
            pl.when(core != owner)(lambda: pair_copy(index).wait_send())
        owned(index, act)

    def side_stage(index):
        name, _, start, rows, left, cols = chunks[index]
        half = rows // 2
        lanes = slice(left, left + cols)

        def act():
            side_copy(index).wait()
            here = cut(start + side * half, half)
            arrived = sides[name][cut(start // 2, half), lanes].astype(F32)
            sums[name][here, lanes] = (sums[name][here, lanes].astype(F32) + arrived).astype(BF16)
            for hop in range(1, LINE):
                line_copy(index, hop).start()

        owned(index, act)

    def line_stage(index):
        name, _, start, rows, left, cols = chunks[index]
        half, piece = rows // 2, rows // SQUARE
        lanes = slice(left, left + cols)

        def act():
            for hop in range(1, LINE):
                line_copy(index, hop).wait()
            here = cut(start + side * half + line * piece, piece)
            value = sums[name][here, lanes].astype(F32)
            for hop in range(1, LINE):
                value = value + lines[name][hop - 1, cut(start // SQUARE, piece), lanes].astype(F32)
            fulls[name][here, lanes] = value.astype(BF16)
            for hop in range(1, LINE):
                back_copy(index, hop).start()

        owned(index, act)

    def back_stage(index):
        def act():
            for hop in range(1, LINE):
                back_copy(index, hop).wait()
            full_copy(index).start()

        owned(index, act)

    def full_stage(index):
        def act():
            full_copy(index).wait()
            for copy in result_copies(index):
                copy.start()

        owned(index, act)

    def result_wait(index):
        for copy in result_copies(index):
            copy.wait()

    stages = {
        "pair": pair_stage,
        "side": side_stage,
        "line": line_stage,
        "back": back_stage,
        "full": full_stage,
    }

    def rows_copy(hop):
        target = across(hop)
        return remote(
            rows_buf.at[cut(target * quarter, quarter), :],
            parts_ref.at[section],
            rows_send.at[hop],
            rows_recv.at[hop],
            (target, group),
        )

    def load_copies():
        pairs = [
            (out_ref, out_grad),
            (up_ref, up_grad),
            (down_ref, down_grad),
            (small_ref, small_grad),
        ]
        pairs += [
            (even_ref.at[:, origin], even_grad.at[:, target]) for origin, target in regroup()
        ]
        return [
            pltpu.make_async_copy(origin, target, load_sem.at[index])
            for index, (origin, target) in enumerate(pairs)
        ]

    def regroup():
        for pair in range(width // LANES):
            for place in range(3):
                yield (
                    pl.ds(place * width + pair * LANES, LANES),
                    pl.ds((3 * pair + place) * LANES, LANES),
                )

    def kept_copies(members=range(5)):
        pairs = (
            (middle_src, middle_ref),
            (attended_src, attended_ref),
            (out_weight_src, out_weight_ref),
            (hidden_src, hidden_ref),
            (key_mark_src, key_mark_ref),
        )
        return [
            pltpu.make_async_copy(*pairs[member], local_sem.at[1 + member]) for member in members
        ]

    def early_copies(members):
        pairs = (
            (grouped_src, grouped_ref),
            (proj_src, proj_ref),
            (keep_src, keep_ref),
            (added_src, added_ref),
            (long_src, sent_long),
        )
        return [
            pltpu.make_async_copy(*pairs[member], early_sem.at[member]) for member in members
        ]

    def early_wait(*members):
        for copy in early_copies(members):
            copy.wait()

    def long_copy():
        return remote(
            sent_long, added_ref, short_send.at[1], short_recv.at[1], (across(2), group)
        )

    def kept_wait(*members):
        for copy in kept_copies(members):
            copy.wait()

    @pl.when(step == 0)
    def _():
        @pl.when(chip == 0)
        def _():
            for copy in early_copies(range(5)):
                copy.start()
            for copy in kept_copies():
                copy.start()
            small_grad[...] = jnp.zeros_like(small_grad)

        @pl.when(chip == 1)
        def _():
            pltpu.make_async_copy(pooled_grad_ref, sent_rows, local_sem.at[0]).start()
            pltpu.make_async_copy(short_result_ref, short_rows, local_sem.at[6]).start()
            for copy in early_copies(range(3)):
                copy.start()
            for copy in load_copies():
                copy.start()

        barrier_with(
            [(across(hop), group) for hop in range(1, 4)]
            + [neighbour]
            + [along(hop) for hop in range(1, LINE)]
        )
        short_copy = remote(
            sent_rows, short_rows, short_send.at[0], short_recv.at[0], (across(2), group)
        )

        @pl.when(chip == 0)
        def _():
            early_wait(4)
            long_copy().start()
            early_wait(3)
            short_copy.wait_recv()

        @pl.when(chip == 1)
        def _():
            pltpu.make_async_copy(pooled_grad_ref, sent_rows, local_sem.at[0]).wait()
            short_copy.start()
            pltpu.make_async_copy(short_result_ref, short_rows, local_sem.at[6]).wait()

        early_wait(0, 1, 2)
        rows = short_rows[...]
        flip = rows.T
        for place in range(3):
            lanes = slice(place * width, (place + 1) * width)
            odd_grad[:, lanes] = dot(flip, grouped_ref[:, lanes], 1, 0).astype(BF16)
            pair_start(place)
        for place in range(3):
            lanes = slice(place * width, (place + 1) * width)
            spread_rows = dot(rows, proj_ref[width : 2 * width, lanes], 1, 0)
            factor = jnp.maximum(keep_ref[place], chip.astype(F32))
            for part in range(groups):
                moved[part, pl.ds(place, short, stride=3), :] = (
                    spread_rows[:, part * LANES : (part + 1) * LANES] * factor
                )
        for part in range(groups):
            moved[part, length:, :] = jnp.zeros((8, LANES), F32)

        @pl.when(chip == 0)
        def _():
            for part in range(groups):
                lanes = slice(part * LANES, (part + 1) * LANES)
                rows_buf[:, lanes] = (
                    added_ref[:, lanes].astype(F32) + moved[part, 2 : 2 + length, :]
                ).astype(BF16)

        @pl.when(chip == 1)
        def _():
            for copy in load_copies():
                copy.wait()
            short_copy.wait_send()

    for tick, events in TICKS.items():

        @pl.when(step == tick)
        def _():
            for stage, index in events:
                stages[stage](index)

    @pl.when((chip == 0) & (step == 1))
    def _():
        kept_wait(0)
        for rows in row_cuts(length, stride):
            standard, _ = standardize(middle_ref[rows, :])
            normal[:, rows] = (standard * gain_ref[8:9, :]).astype(BF16).T
            grad_flip[:, rows] = rows_buf[rows, :].T
            total[rows, :] = jnp.zeros((stride, width), F32)

    @pl.when((chip == 0) & (step >= 1) & (step < first_head))
    def _():
        turn = step - 1
        part = (turn % 2) * 2 + turn // 2
        span = pl.ds(pl.multiple_of(part * 512, 512), 512)
        down_grad[span, :] = dot(grad_flip[...], active_ref[...], 1, 0).astype(BF16).T

    for tick, events in MIDDLES.items():

        @pl.when(step == tick)
        def _():
            for stage, index in events:
                stages[stage](index)

    @pl.when((chip == 0) & (step >= 1) & (step < first_head))
    def _():
        turn = step - 1
        part = (turn % 2) * 2 + turn // 2
        span = pl.ds(pl.multiple_of(part * 512, 512), 512)
        for rows in row_cuts(length, stride):
            grad_active = dot(rows_buf[rows, :], down_weight_ref[...], 1, 1)
            low = (grad_active * slant_ref[rows, :].astype(F32)).astype(BF16)
            lower[rows, :] = low
            total[rows, :] += dot(low, up_weight_ref[...], 1, 1)
        up_grad[:, span] = dot(normal[...], lower[...], 1, 0).astype(BF16)

    @pl.when((chip == 0) & (step == first_head - 1))
    def _():
        kept_wait(1, 2)
        gain_sum = jnp.zeros((1, width), F32)
        for rows in row_cuts(length, stride):
            standard, inverse = standardize(middle_ref[rows, :])
            grad = total[rows, :]
            gain_sum = gain_sum + jnp.sum(grad * standard, axis=0, keepdims=True)
            middle_grad = rows_buf[rows, :].astype(F32) + norm_back(
                grad, gain_ref[8:9, :], standard, inverse
            )
            total[rows, :] = middle_grad
            low = middle_grad.astype(BF16)
            lower[rows, :] = low
            attended_grad[rows, :] = dot(low, out_weight_ref[...], 1, 1).astype(BF16)
        small_grad[1:2, :] = gain_sum
        out_grad[...] = dot(attended_ref[...], lower[...], 0, 0).astype(BF16)

    @pl.when((chip == 0) & (step == first_head))
    def _():
        kept_wait(3, 4)
        for rows in row_cuts(length, stride):
            standard, _ = standardize(hidden_ref[rows, :].astype(F32))
            normal[:, rows] = (standard * gain_ref[0:1, :]).astype(BF16).T

    @pl.when((chip == 0) & (step >= first_head) & (step < last))
    def _():
        head = step - first_head
        cuts = head_cuts(head // 2, width)
        slope_grad = head_back(
            head % 2, key_mark_ref, query_ref, key_ref, value_ref, attended_ref.at[:, cuts[0]],
            attended_grad.at[:, cuts[0]], mixed, keys, values, grads, key_sum, value_sum,
            cuts, tile,
        )
        column = lax.broadcasted_iota(jnp.int32, (1, width), 1)
        small_grad[2:3, :] += jnp.where(column == head, slope_grad, 0.0)

    @pl.when((chip == 0) & (step >= first_head) & (step < last) & (step % 2 == 0))
    def _():
        pair = (step - first_head) // 2
        for place, span in enumerate(head_cuts(pair, width)):
            target = pl.ds(pl.multiple_of((3 * pair + place) * LANES, LANES), LANES)
            even_grad[:, target] = dot(normal[...], mixed[:, span], 1, 0).astype(BF16)

    for begin, members in BEGINS.items():
        @pl.when(step == begin)
        def _():
            for index in members:
                pair_start(index)

    @pl.when((chip == 0) & (step == last))
    def _():
        gain_sum = jnp.zeros((1, width), F32)
        for rows in row_cuts(length, stride):
            standard, inverse = standardize(hidden_ref[rows, :].astype(F32))
            grad = dot(mixed[rows, :], proj_ref[0:width, :], 1, 1)
            gain_sum = gain_sum + jnp.sum(grad * standard, axis=0, keepdims=True)
            rows_buf[rows, :] = (
                total[rows, :] + norm_back(grad, gain_ref[0:1, :], standard, inverse)
            ).astype(BF16)
        small_grad[0:1, :] = gain_sum

    @pl.when((chip == 0) & (step == last))
    def _():
        long_copy().wait_send()

    @pl.when((chip == 1) & (step == last))
    def _():
        long_copy().wait_recv()
        for part in range(groups):
            lanes = slice(part * LANES, (part + 1) * LANES)
            rows_buf[:, lanes] = (
                added_ref[:, lanes].astype(F32) + moved[part, 0:length, :]
            ).astype(BF16)

    @pl.when(step == last)
    def _():
        small_one = remote(small_grad, small_pair, small_send.at[0], small_recv.at[0], partner)
        small_one.start()
        for hop in range(1, 4):
            rows_copy(hop).start()
        parts_ref[section] = rows_buf[cut(section * quarter, quarter), :]
        for stage, index in DRAIN[:3]:
            stages[stage](index)
        small_one.wait()
        small_full[...] = small_grad[...] + small_pair[...]
        small_two = remote(small_full, small_side, small_send.at[1], small_recv.at[1], neighbour)
        small_two.start()
        for stage, index in DRAIN[3:7]:
            stages[stage](index)
        small_two.wait()
        small_full[...] = small_full[...] + small_side[...]
        small_rest = [
            remote(
                small_full,
                small_line.at[line],
                small_send.at[1 + hop],
                small_recv.at[1 + hop],
                along(hop),
            )
            for hop in range(1, LINE)
        ]
        for copy in small_rest:
            copy.start()
        for stage, index in DRAIN[7:]:
            stages[stage](index)
        for copy in small_rest:
            copy.wait()
        small_line[line] = small_full[...]
        small_result[...] = (small_line[0] + small_line[1]) + (small_line[2] + small_line[3])
        for hop in range(1, 4):
            rows_copy(hop).wait()
        parts_copy = pltpu.make_async_copy(parts_ref, parts_result, result_sem.at[len(chunks), 0])
        parts_copy.start()
        for index in range(len(chunks)):
            owned(index, functools.partial(result_wait, index))
        parts_copy.wait()


def last_call(
    hidden, gains, proj, key_mark, middle, attended, out_weight, keep, grouped, added,
    active, slant, up_weight, down_weight, query, keyval,
    long_rows, pooled_grad, short_result, even, out_grad, up_grad, down_grad, small, tile,
):
    inside = pl.BlockSpec(memory_space=pltpu.VMEM)
    anywhere = pl.BlockSpec(memory_space=pl.ANY)
    length, width = hidden.shape
    short = length // 3
    heads = query.shape[0]
    units = up_weight.shape[1]
    wide = even.shape[1]
    piece = units // PARTS
    half = lambda value: (value.shape[0] // 2, value.shape[1])
    shapes = [even.shape, half(out_grad), half(up_grad), half(down_grad)]
    count = len(chunk_list())
    vmem = pltpu.VMEM
    scaled = lambda over: [vmem((rows // over, cols), BF16) for rows, cols in shapes]
    semaphores = lambda *shape: [pltpu.SemaphoreType.DMA(shape)] * 2

    def part_of(step):
        turn = jnp.clip(step - 1, 0, PARTS - 1)
        return turn % 2 * 2 + turn // 2

    def head_of(step):
        return jnp.clip(step - 1 - PARTS, 0, heads - 1)

    column = lambda start: pl.BlockSpec(
        (length, LANES), lambda step: (0, start + head_of(step) // 2)
    )
    results = pl.pallas_call(
        functools.partial(last_kernel, tile=tile),
        grid=(2 + PARTS + heads,),
        in_specs=[anywhere, inside] + [anywhere] * 8
        + [pl.BlockSpec((length, piece), lambda step: (0, part_of(step)))] * 2
        + [
            pl.BlockSpec((width, piece), lambda step: (0, part_of(step))),
            pl.BlockSpec((piece, width), lambda step: (part_of(step), 0)),
            pl.BlockSpec((1, length, LANES), lambda step: (head_of(step), 0, 0)),
            column(0),
            column(heads // 2),
        ]
        + [anywhere] * 8,
        out_specs=[anywhere] * 4 + [inside, anywhere],
        out_shape=[jax.ShapeDtypeStruct(shape, BF16) for shape in shapes]
        + [
            jax.ShapeDtypeStruct(small.shape, F32),
            jax.ShapeDtypeStruct((4, length // 4, width), BF16),
        ],
        scratch_shapes=[
            vmem((length, width), F32),
            vmem((length, width), BF16),
            vmem((width, width), BF16),
            vmem((length, width), BF16),
            vmem((length, LANES), BF16),
            vmem(proj.shape, BF16),
            vmem(keep.shape, F32),
            vmem(grouped.shape, BF16),
            vmem((length, width), BF16),
            vmem((length, width), BF16),
            vmem((short, width), BF16),
            vmem((short, width), BF16),
            vmem((width // LANES, length + 8, LANES), F32),
            vmem((length, width), BF16),
            vmem((width, length), BF16),
            vmem((width, length), BF16),
            vmem((length, width), F32),
            vmem((length, width), BF16),
            vmem((length, width), BF16),
            vmem((length, 3 * width), BF16),
            vmem((length, LANES), BF16),
            vmem((length, LANES), BF16),
            vmem((length, LANES), BF16),
            vmem((length, LANES), F32),
            vmem((length, LANES), F32),
            vmem((width, wide), BF16),
            vmem((width, wide), BF16),
            vmem(out_grad.shape, BF16),
            vmem(up_grad.shape, BF16),
            vmem(down_grad.shape, BF16),
            vmem(small.shape, F32),
            vmem(small.shape, F32),
            vmem((4, length // 4, width), BF16),
        ]
        + scaled(1)
        + scaled(1)
        + scaled(2)
        + [vmem((LINE - 1, rows // SQUARE, cols), BF16) for rows, cols in shapes]
        + [vmem(small.shape, F32)] * 2
        + [vmem((LINE,) + small.shape, F32)]
        + [pltpu.SemaphoreType.DMA((7,))]
        + semaphores(count)
        + semaphores(count)
        + semaphores(count, LINE - 1)
        + semaphores(count, LINE - 1)
        + semaphores(count)
        + semaphores(2 + LINE - 1)
        + semaphores(4)
        + [pltpu.SemaphoreType.DMA((count + 1, 3)), pltpu.SemaphoreType.DMA((16,))]
        + semaphores(2)
        + [pltpu.SemaphoreType.DMA((5,))],
        compiler_params=pltpu.CompilerParams(
            collective_id=1, has_side_effects=True, vmem_limit_bytes=VMEM_LIMIT
        ),
        name="last",
    )(
        hidden, gains, proj, key_mark, middle, attended, out_weight, keep, grouped, added,
        active, slant, up_weight, down_weight, query, keyval, keyval, long_rows,
        pooled_grad, short_result, even, out_grad, up_grad, down_grad, small,
    )
    parts = results[-1]
    results = results[:-1]
    squares = lax.axis_size("dp") // SQUARE
    if squares > 1:
        members = [
            [number * SQUARE + place for number in range(squares)] for place in range(SQUARE)
        ]
        results = lax.psum(results, "dp", axis_index_groups=members)
    return results, parts


def widen_kernel(*refs):
    step = pl.program_id(0)
    half = pl.num_programs(0) // 2
    core = lax.axis_index("section") % 2
    inputs = len(refs) // 2 - 1
    *sources, parts_ref, small_ref = refs[:inputs]
    *targets, input_ref, results_ref, gain_ref, slope_ref = refs[inputs:]
    mine = jnp.where(core == 0, small_ref[0:1, :], small_ref[1:2, :])
    gain_ref[...] = mine
    per = slope_ref.shape[1]
    slope_ref[...] = jnp.where(core == 0, small_ref[2:3, 0:per], small_ref[2:3, per : 2 * per])
    for source, target in zip(sources, targets):
        target[...] = source[...].astype(F32)

    @pl.when(step < half)
    def _():
        input_ref[...] = parts_ref[...].astype(F32)

    @pl.when(step >= half)
    def _():
        results_ref[...] = parts_ref[...]


def widen_call(grads, parts, small, per):
    width = small.shape[1]
    whole = lambda *shape: pl.BlockSpec(shape, lambda step: (0, 0))
    steps = parts.shape[0]
    half = steps // 2
    block = lambda value: pl.BlockSpec(
        (value.shape[0] // steps, value.shape[1]), lambda step: (step, 0)
    )
    page = (1,) + parts.shape[1:]
    return pl.pallas_call(
        widen_kernel,
        grid=(steps,),
        in_specs=[block(value) for value in grads]
        + [pl.BlockSpec(page, lambda step: (step, 0, 0)), whole(*small.shape)],
        out_specs=[block(value) for value in grads]
        + [
            pl.BlockSpec(page, lambda step: (jnp.minimum(step, half - 1), 0, 0)),
            pl.BlockSpec(page, lambda step: (jnp.maximum(step - half, 0), 0, 0)),
            whole(1, width),
            whole(1, per),
        ],
        out_shape=[jax.ShapeDtypeStruct(value.shape, F32) for value in grads]
        + [
            jax.ShapeDtypeStruct((half,) + parts.shape[1:], F32),
            jax.ShapeDtypeStruct((half,) + parts.shape[1:], BF16),
            jax.ShapeDtypeStruct((1, width), F32),
            jax.ShapeDtypeStruct((1, per), F32),
        ],
        compiler_params=params(),
        name="widen",
    )(*grads, parts, small)


def body(
    activations,
    cotangent,
    article_ids,
    section_proj,
    out_rows,
    up_rows,
    down_rows,
    norm_gains,
    slopes,
):
    section = lax.axis_index("section")
    first_chip = section < 2
    width = activations.shape[3]
    length = article_ids.shape[2]
    short = length // 3
    heads = 2 * slopes.shape[1]
    tile = length // 3

    (
        row, proj, out_weight, up_weight, down_weight, query, keyval, attended, middle, active,
        slant, grouped, long_rows, pooled, short_grad, added, gains, key_mark, short_query_mark,
        short_key_mark, keep,
    ) = first_call(
        activations, cotangent, article_ids, norm_gains, slopes, section_proj[0], out_rows,
        up_rows, down_rows, heads, tile,
    )

    def zeros_of(call, *operands):
        return jax.tree.map(
            lambda leaf: jnp.zeros(leaf.shape, leaf.dtype), jax.eval_shape(call, *operands)
        )

    def short_all(pooled, grad):
        return short_call(
            pooled, grad, gains, short_query_mark, short_key_mark, proj, out_weight, up_weight,
            down_weight, heads,
        )

    short_result, pooled_grad, *short_grads = lax.cond(
        first_chip,
        lambda *operands: zeros_of(short_all, *operands),
        short_all,
        pooled,
        short_grad,
    )
    (proj_grad, out_grad, up_grad, down_grad, small), parts = last_call(
        row, gains, proj, key_mark, middle, attended, out_weight, keep, grouped, added,
        active, slant, up_weight, down_weight, query, keyval,
        long_rows, pooled_grad, short_result, *short_grads, tile=tile,
    )
    proj_grad, out_grad, up_grad, down_grad, input_grad, results, gain_grad, slope_grad = (
        widen_call((proj_grad, out_grad, up_grad, down_grad), parts, small, heads // 2)
    )
    return (
        results[:, None],
        input_grad[:, None],
        proj_grad[None],
        out_grad,
        up_grad,
        down_grad,
        gain_grad,
        slope_grad,
    )


def solution(mesh):
    return jax.shard_map(
        body,
        mesh=mesh,
        in_specs=(
            P(None, "dp", "section", None),
            P(None, "dp", "section", None),
            P(None, "dp", None),
            P("section", None, None),
            P("section", None),
            P("section", None),
            P("section", None),
            P("section", None),
            P("section", None),
        ),
        out_specs=(
            P(None, "dp", "section", None),
            P(None, "dp", "section", None),
            P("section", None, None),
            P("section", None),
            P("section", None),
            P("section", None),
            P("section", None),
            P("section", None),
        ),
        check_vma=False,
    )
```

```python
import functools

import jax
import jax.numpy as jnp
from jax import lax
from jax.experimental import pallas as pl
from jax.experimental.pallas import tpu as pltpu
from jax.sharding import PartitionSpec as P

EPSILON = 1e-05
APART = -1e30
F32 = jnp.float32
BF16 = jnp.bfloat16
VMEM_LIMIT = 60 * 1024 * 1024
LANES = 128
PARTS = 4
HALF = 64
MESH = pl.DeviceIdType.MESH


def dot(left, right, left_dim, right_dim):
    return lax.dot_general(
        left, right, (((left_dim,), (right_dim,)), ((), ())), preferred_element_type=F32
    )


def standardize(value):
    centred = value - jnp.mean(value, axis=-1, keepdims=True)
    inverse = lax.rsqrt(jnp.mean(centred * centred, axis=-1, keepdims=True) + EPSILON)
    return centred * inverse, inverse


def norm_back(grad, gain, standard, inverse):
    scaled = grad * gain
    centred = (
        scaled
        - jnp.mean(scaled, axis=-1, keepdims=True)
        - standard * jnp.mean(scaled * standard, axis=-1, keepdims=True)
    )
    return centred * inverse


def params(limit=VMEM_LIMIT):
    return pltpu.CompilerParams(vmem_limit_bytes=limit)


def row_cuts(length, step):
    return [slice(start, start + step) for start in range(0, length, step)]


def lane_ids(rows):
    return lax.broadcasted_iota(jnp.int32, (rows, LANES), 1)


def barrier_with(devices):
    barrier = pltpu.get_barrier_semaphore()
    for device in devices:
        pl.semaphore_signal(barrier, inc=1, device_id=device, device_id_type=MESH)
    pl.semaphore_wait(barrier, len(devices))


def make_marks(wide, lane):
    length = wide.shape[0]
    mark = lane % HALF
    position = lax.broadcasted_iota(jnp.int32, (length, LANES), 0)
    low = position % 256
    same = wide == (mark - 2).astype(F32)
    chosen = (mark >= 2) & (mark < 5)
    query = jnp.where(chosen & same, 1.0, 0.0)
    fixed = jnp.where(mark < 8, 1.0, 0.0)
    apart = jnp.where(same, 0.0, APART)
    key = jnp.where(chosen, apart, fixed)
    key = jnp.where(mark == 0, low.astype(F32), key)
    key = jnp.where(mark == 1, (position - low).astype(F32), key)
    return query.astype(BF16), key.astype(BF16)


def gelu_pieces(value):
    root = 0.7978845608028654
    square = value * value
    inner = jnp.tanh(value * (root + (root * 0.044715) * square))
    half = 0.5 + 0.5 * inner
    active = value * half
    slant = half + active * (1.0 - inner) * (root + (3.0 * root * 0.044715) * square)
    return active, slant


LINE = 4
SQUARE = 2 * LINE


def head_back(
    side,
    key_mark_ref,
    query_ref,
    key_ref,
    value_ref,
    attended_ref,
    attended_grad_ref,
    mixed,
    keys,
    values,
    grads,
    key_sum,
    value_sum,
    cuts,
    tile,
):
    length = key_ref.shape[0]
    blocks = length // tile
    lane = lane_ids(tile)
    here = lane // HALF == side
    mark = lane % HALF
    earlier = lax.broadcasted_iota(jnp.int32, (tile, tile), 0) <= lax.broadcasted_iota(
        jnp.int32, (tile, tile), 1
    )
    position = lax.broadcasted_iota(jnp.int32, (tile, LANES), 0)
    spans = [slice(block * tile, (block + 1) * tile) for block in range(blocks)]
    for rows in spans:
        grad = attended_grad_ref[rows, :].astype(F32)
        product = jnp.where(here, grad * attended_ref[rows, :].astype(F32), 0.0)
        keys[rows, :] = jnp.where(
            here, key_ref[rows, :].astype(F32), key_mark_ref[rows, :].astype(F32)
        ).astype(BF16)
        values[rows, :] = jnp.where(here, value_ref[rows, :].astype(F32), 1.0).astype(BF16)
        centre = -jnp.sum(product, axis=1, keepdims=True)
        first = centre.astype(BF16).astype(F32)
        second = (centre - first).astype(BF16).astype(F32)
        third = centre - first - second
        marks = jnp.where(
            mark == 0, first, jnp.where(mark == 1, second, jnp.where(mark == 2, third, 0.0))
        )
        grads[rows, :] = jnp.where(here, grad, marks).astype(BF16)

    def score(block, other):
        rows, cols = spans[block], spans[other]
        raw = dot(keys[cols, :], query_ref[0, rows, :], 1, 1)
        return raw, dot(values[cols, :], grads[rows, :], 1, 1)

    def finish(block, other, raw, pull):
        rows, cols = spans[block], spans[other]
        weights = jnp.exp(raw)
        if other == block:
            weights = jnp.where(earlier, weights, 0.0)
        change = (weights * pull).astype(BF16)
        key_term = dot(change, query_ref[0, rows, :], 1, 0)
        value_term = dot(weights.astype(BF16), grads[rows, :], 1, 0)
        if other == block:
            key_sum[cols, :] = key_term
            value_sum[cols, :] = value_term
        else:
            key_sum[cols, :] += key_term
            value_sum[cols, :] += value_term
        return dot(change, keys[cols, :], 0, 0)

    def keep(rows, cut, value):
        mixed[rows, cut] = jnp.where(here, value, mixed[rows, cut].astype(F32)).astype(BF16)

    order = [(block, other) for block in range(blocks) for other in range(block + 1)]
    ahead = score(*order[0])
    slope_sum = jnp.zeros((tile, LANES), F32)
    total = None
    for index, (block, other) in enumerate(order):
        now = ahead
        if index + 1 < len(order):
            ahead = score(*order[index + 1])
        term = finish(block, other, *now)
        total = term if other == 0 else total + term
        if other == block:
            place = -(position + block * tile).astype(F32)
            slope_sum = slope_sum + jnp.where(
                mark < 2, total, jnp.where(mark == 5, total * place, 0.0)
            )
            keep(spans[block], cuts[0], total * 0.125)
    for rows in spans:
        keep(rows, cuts[1], key_sum[rows, :])
        keep(rows, cuts[2], value_sum[rows, :])
    return jnp.sum(jnp.where(here, 0.0, slope_sum))


def head_cuts(pair, width):
    return [
        pl.ds(pl.multiple_of(place * width + pair * LANES, LANES), LANES) for place in range(3)
    ]


def first_kernel(
    act_ref,
    cot_ref,
    ids_ref,
    gain_ref,
    slope_ref,
    proj_src,
    out_src,
    up_src,
    down_src,
    row_dst,
    proj_dst,
    out_dst,
    up_dst,
    down_dst,
    query_dst,
    keyval_dst,
    attended_dst,
    middle_dst,
    active_dst,
    slant_dst,
    grouped_dst,
    long_dst,
    pooled_dst,
    back_dst,
    added_dst,
    small_all,
    key_mark,
    short_query_mark,
    short_key_mark,
    keep_ref,
    row_ref,
    proj_all,
    out_all,
    up_all,
    down_all,
    query_mark,
    wide_ref,
    mixed,
    queries,
    keys,
    values,
    attended,
    middle,
    actives,
    slants,
    moved,
    grouped,
    result,
    pooled_own,
    pooled,
    back,
    added,
    load_sem,
    row_send,
    row_recv,
    pair_send,
    pair_recv,
    pool_send,
    pool_recv,
    done_sem,
    cot_send,
    cot_recv,
    *,
    tile,
    heads,
):
    section = lax.axis_index("section")
    group = lax.axis_index("dp")
    sections = 4
    core = section % 2
    chip = section // 2
    partner = chip * 2 + (1 - core)
    quarter, width = act_ref.shape[2:]
    length = row_ref.shape[0]
    short = length // 3
    groups = width // LANES
    units = up_all.shape[1]
    piece = units // PARTS
    blocks = length // tile

    def span_of(whole):
        rows = whole.shape[0] // 2
        return pl.ds(pl.multiple_of(core * rows, rows), rows)

    wholes = (proj_all, small_all, out_all, up_all, down_all)
    shards = (proj_src, None, out_src, up_src, down_src)

    def load_copy(index):
        return pltpu.make_async_copy(
            shards[index], wholes[index].at[span_of(wholes[index]), :], load_sem.at[index]
        )

    for index in (0, 2, 3, 4):
        load_copy(index).start()
    small_rows = span_of(small_all)
    small_all[small_rows, :] = jnp.concatenate(
        [
            gain_ref[...].astype(F32),
            jnp.concatenate(
                [
                    slope_ref[...].astype(F32),
                    jnp.zeros((1, width - slope_ref.shape[1]), F32),
                ],
                axis=1,
            ),
            jnp.zeros((6, width), F32),
        ],
        axis=0,
    )
    others = [lax.rem(section + hop, sections) for hop in range(1, sections)]
    barrier_with([(other, group) for other in others])
    place = pl.ds(pl.multiple_of(section * quarter, quarter), quarter)

    def row_copy(source_ref, hop):
        target = lax.rem(section + hop, sections)
        return pltpu.make_async_remote_copy(
            src_ref=source_ref.at[target % 2, 0],
            dst_ref=row_ref.at[place, :],
            send_sem=row_send.at[hop],
            recv_sem=row_recv.at[hop],
            device_id=(target, group),
            device_id_type=MESH,
        )

    for hop in (2, 1, 3):
        target_chip = lax.rem(section + hop, sections) // 2

        @pl.when(target_chip == 0)
        def _():
            row_copy(act_ref, hop).start()

        @pl.when(target_chip == 1)
        def _():
            row_copy(cot_ref, hop).start()

    def pair_copy(index):
        spot = wholes[index].at[span_of(wholes[index]), :]
        return pltpu.make_async_remote_copy(
            src_ref=spot,
            dst_ref=spot,
            send_sem=pair_send.at[index],
            recv_sem=pair_recv.at[index],
            device_id=(partner, group),
            device_id_type=MESH,
        )

    for index in range(len(wholes)):
        if shards[index] is not None:
            load_copy(index).wait()
        pair_copy(index).start()

    @pl.when(chip == 0)
    def _():
        row_ref[place, :] = act_ref[core, 0]

    @pl.when(chip == 1)
    def _():
        row_ref[place, :] = cot_ref[core, 0]

    ids = jnp.broadcast_to(ids_ref[core].astype(F32), (LANES, length))
    wide = ids.T
    wide_ref[0:8, :] = jnp.full((8, LANES), -1.0, F32)
    wide_ref[8:, :] = wide
    query_mark[...], key_mark[...] = make_marks(wide, lane_ids(length))
    short_wide = wide_ref[pl.ds(8, short, stride=3), :]
    short_query_mark[...], short_key_mark[...] = make_marks(short_wide, lane_ids(short))
    for turn in range(3):
        current = wide_ref[pl.ds(8 + turn, short, stride=3), :]
        before = wide_ref[pl.ds(6 + turn, short, stride=3), :]
        keep_ref[turn] = jnp.where(current == before, 1.0, 0.0)
    pair_copy(0).wait_recv()
    pair_copy(1).wait_recv()

    @pl.when(core == 0)
    def _():
        row_copy(act_ref, 3).wait_recv()

    @pl.when(core == 1)
    def _():
        row_copy(act_ref, 1).wait_recv()

    lane = lane_ids(tile)
    upper = lane >= HALF
    mark = lane % HALF
    sides = (jnp.logical_not(upper), upper)
    earlier = lax.broadcasted_iota(jnp.int32, (tile, tile), 0) >= lax.broadcasted_iota(
        jnp.int32, (tile, tile), 1
    )
    spans = [slice(block * tile, (block + 1) * tile) for block in range(blocks)]

    def project(rows):
        standard, _ = standardize(row_ref[rows, :].astype(F32))
        normal = (standard * small_all[0:1, :]).astype(BF16)
        mixed[rows, :] = dot(normal, proj_all[0:width, :], 1, 0).astype(BF16)

    def attend(members):
        def attend_pair(pair, carry):
            cuts = head_cuts(pair, width)
            column = lax.broadcasted_iota(jnp.int32, (1, width), 1)
            per = heads // 2
            slope_of = []
            for side in range(2):
                number = 2 * pair + side
                slopes = jnp.where(number < per, small_all[1:2, :], small_all[9:10, :])
                slope_of.append(
                    jnp.sum(
                        jnp.where(column == number % per, slopes, 0.0), axis=1, keepdims=True
                    )
                )
            for block in members:
                rows = spans[block]
                key_rows = mixed[rows, cuts[1]].astype(F32)
                value_rows = mixed[rows, cuts[2]].astype(F32)
                marks = key_mark[rows, :].astype(F32)
                for side, here in enumerate(sides):
                    keys[2 * pair + side, rows, :] = jnp.where(here, key_rows, marks).astype(BF16)
                    values[2 * pair + side, rows, :] = jnp.where(here, value_rows, 1.0).astype(
                        BF16
                    )

            def score(block, side):
                rows = spans[block]
                marks = jnp.where(mark < 2, slope_of[side], query_mark[rows, :].astype(F32))
                query = jnp.where(sides[side], mixed[rows, cuts[0]].astype(F32) * 0.125, marks)
                query = query.astype(BF16)
                number = 2 * pair + side
                near = jnp.where(earlier, dot(query, keys[number, rows, :], 1, 1), APART)
                far = dot(query, keys[number, : block * tile, :], 1, 1) if block else None
                return query, near, far

            def finish(block, side, query, near, far):
                rows = spans[block]
                number = 2 * pair + side
                highest = jnp.max(near, axis=1, keepdims=True)
                if block:
                    highest = jnp.maximum(highest, jnp.max(far, axis=1, keepdims=True))
                mass = dot(jnp.exp(near - highest).astype(BF16), values[number, rows, :], 1, 0)
                if block:
                    mass = mass + dot(
                        jnp.exp(far - highest).astype(BF16),
                        values[number, : block * tile, :],
                        1,
                        0,
                    )
                level = -(highest + jnp.log(mass))
                first = level.astype(BF16).astype(F32)
                second = (level - first).astype(BF16).astype(F32)
                third = level - first - second
                query = query.astype(F32)
                level_marks = jnp.where(
                    mark == 5,
                    first,
                    jnp.where(mark == 6, second, jnp.where(mark == 7, third, query)),
                )
                queries[number, rows, :] = jnp.where(sides[side], query, level_marks).astype(BF16)
                return mass / pltpu.roll(mass, HALF, 1)

            order = [(block, side) for block in members for side in range(2)]
            ahead = score(*order[0])
            shares = [None, None]
            for index, (block, side) in enumerate(order):
                now = ahead
                if index + 1 < len(order):
                    ahead = score(*order[index + 1])
                shares[side] = finish(block, side, *now)
                if side:
                    attended[spans[block], cuts[0]] = jnp.where(
                        upper, shares[1], shares[0]
                    ).astype(BF16)
            return carry

        lax.fori_loop(0, heads // 2, attend_pair, 0)

    def rows_wait_rest():
        row_copy(act_ref, 2).wait_recv()

        @pl.when(core == 0)
        def _():
            row_copy(act_ref, 1).wait_recv()

        @pl.when(core == 1)
        def _():
            row_copy(act_ref, 3).wait_recv()

    def pool_copy(block):
        rows = pl.ds(block * (tile // 3), tile // 3)
        return pltpu.make_async_remote_copy(
            src_ref=pooled_own.at[rows, :],
            dst_ref=pooled.at[rows, :],
            send_sem=pool_send.at[block],
            recv_sem=pool_recv.at[block],
            device_id=(lax.rem(section + 2, sections), group),
            device_id_type=MESH,
        )

    def out_copies(members=range(6)):
        kept = [
            (proj_all, proj_dst),
            (out_all, out_dst),
            (up_all, up_dst),
            (down_all, down_dst),
            (row_ref, row_dst),
            (grouped, grouped_dst),
        ]
        return [
            pltpu.make_async_copy(*kept[member], done_sem.at[member]) for member in members
        ]

    def attend_copies():
        kept = [
            (queries, query_dst),
            (mixed.at[:, pl.ds(width, 2 * width)], keyval_dst),
            (attended, attended_dst),
        ]
        return [
            pltpu.make_async_copy(origin, target, done_sem.at[6 + index])
            for index, (origin, target) in enumerate(kept)
        ]

    def tile_copies(block):
        rows = pl.ds(block * tile, tile)
        kept = [(middle, middle_dst), (actives, active_dst), (slants, slant_dst), (result, long_dst)]
        return [
            pltpu.make_async_copy(
                origin.at[rows, :], target.at[rows, :], done_sem.at[9 + 4 * block + index]
            )
            for index, (origin, target) in enumerate(kept)
        ]

    def dense_tile(block):
        rows = spans[block]
        value = row_ref[rows, :].astype(F32) + dot(attended[rows, :], out_all[...], 1, 0)
        middle[rows, :] = value
        standard, _ = standardize(value)
        normal = (standard * small_all[8:9, :]).astype(BF16)
        for part in range(PARTS):
            span = slice(part * piece, (part + 1) * piece)
            active, slant = gelu_pieces(dot(normal, up_all[:, span], 1, 0))
            active = active.astype(BF16)
            actives[rows, span] = active
            slants[rows, span] = slant.astype(BF16)
            value = value + dot(active, down_all[span, :], 1, 0)
        low = value.astype(BF16)
        result[rows, :] = low
        for copy in tile_copies(block):
            copy.start()
        small_tile = tile // 3
        for part in range(groups):
            lanes = slice(part * LANES, (part + 1) * LANES)
            moved[part, 8 + block * tile : 8 + (block + 1) * tile, :] = low[:, lanes].astype(
                F32
            )
        total = None
        small_rows = slice(block * small_tile, (block + 1) * small_tile)
        for turn in range(3):
            picked = jnp.concatenate(
                [
                    moved[part, pl.ds(6 + turn + block * tile, small_tile, stride=3), :]
                    for part in range(groups)
                ],
                axis=1,
            )
            factor = jnp.concatenate([keep_ref[turn, small_rows, :]] * groups, axis=1)
            picked = (picked * factor).astype(BF16)
            cut = slice(turn * width, (turn + 1) * width)
            grouped[small_rows, cut] = picked
            term = dot(picked, proj_all[width : 2 * width, cut], 1, 1)
            total = term if total is None else total + term
        pooled_own[small_rows, :] = total.astype(BF16)
        pool_copy(block).start()

    def cot_copy():
        return pltpu.make_async_remote_copy(
            src_ref=row_ref,
            dst_ref=added,
            send_sem=cot_send.at[0],
            recv_sem=cot_recv.at[0],
            device_id=(lax.rem(section + 2, sections), group),
            device_id_type=MESH,
        )

    @pl.when(chip == 0)
    def _():
        for start in range(0, 2 * quarter, quarter):
            project(slice(start, start + quarter))
        attend((0,))
        for part in range(groups):
            moved[part, 0:8, :] = jnp.zeros((8, LANES), F32)

    for index in range(2, len(wholes)):
        pair_copy(index).wait_recv()

    @pl.when(chip == 0)
    def _():
        dense_tile(0)

    rows_wait_rest()

    @pl.when(chip == 1)
    def _():
        cot_copy().start()

    for copy in out_copies(range(5)):
        copy.start()

    @pl.when(chip == 0)
    def _():
        for start in range(2 * quarter, length, quarter):
            project(slice(start, start + quarter))
        attend(tuple(range(1, blocks)))
        for copy in attend_copies():
            copy.start()
        for block in range(1, blocks):
            dense_tile(block)

    @pl.when(chip == 1)
    def _():
        for part in range(groups):
            lanes = slice(part * LANES, (part + 1) * LANES)
            moved[part, 8:, :] = row_ref[:, lanes].astype(F32)
        for turn in range(3):
            for part in range(groups):
                left = turn * width + part * LANES
                grouped[:, left : left + LANES] = moved[
                    part, pl.ds(8 + turn, short, stride=3), :
                ].astype(BF16)
        back[...] = dot(grouped[...], proj_all[width : 2 * width, :], 1, 1).astype(BF16)
        back_copy = pltpu.make_async_copy(back, back_dst, done_sem.at[21])
        back_copy.start()
        back_copy.wait()
        for block in range(blocks):
            pool_copy(block).wait_recv()
        pooled_copy = pltpu.make_async_copy(pooled, pooled_dst, done_sem.at[23])
        pooled_copy.start()
        pooled_copy.wait()
        cot_copy().wait_send()

    out_copies([5])[0].start()

    @pl.when(chip == 0)
    def _():
        for copy in attend_copies():
            copy.wait()
        for block in range(blocks):
            for copy in tile_copies(block):
                copy.wait()
            pool_copy(block).wait_send()
        cot_copy().wait_recv()
        added_copy = pltpu.make_async_copy(added, added_dst, done_sem.at[22])
        added_copy.start()
        added_copy.wait()

    for copy in out_copies():
        copy.wait()
    for index in range(len(wholes)):
        pair_copy(index).wait_send()
    for hop in range(1, sections):
        row_copy(act_ref, hop).wait_send()


def first_call(
    activations, cotangent, ids, gains, slopes, proj, out_rows, up_rows, down_rows, heads, tile
):
    inside = pl.BlockSpec(memory_space=pltpu.VMEM)
    anywhere = pl.BlockSpec(memory_space=pl.ANY)
    quarter, width = activations.shape[2:]
    length = 4 * quarter
    short = length // 3
    units = up_rows.shape[1]
    shape = jax.ShapeDtypeStruct
    vmem = pltpu.VMEM
    twice = lambda value: (2 * value.shape[0], value.shape[1])
    weights = [twice(value) for value in (proj, out_rows, up_rows, down_rows)]
    return pl.pallas_call(
        functools.partial(first_kernel, tile=tile, heads=heads),
        in_specs=[inside] * 5 + [anywhere] * 4,
        out_specs=[anywhere] * 16 + [inside] * 5,
        out_shape=[shape((length, width), BF16)]
        + [shape(size, BF16) for size in weights]
        + [
            shape((heads, length, LANES), BF16),
            shape((length, 2 * width), BF16),
            shape((length, width), BF16),
            shape((length, width), F32),
            shape((length, units), BF16),
            shape((length, units), BF16),
            shape((short, 3 * width), BF16),
            shape((length, width), BF16),
            shape((short, width), BF16),
            shape((short, width), BF16),
            shape((length, width), BF16),
            shape((16, width), F32),
            shape((length, LANES), BF16),
            shape((short, LANES), BF16),
            shape((short, LANES), BF16),
            shape((3, short, LANES), F32),
        ],
        scratch_shapes=[vmem((length, width), BF16)]
        + [vmem(size, BF16) for size in weights]
        + [
            vmem((length, LANES), BF16),
            vmem((length + 8, LANES), F32),
            vmem((length, 3 * width), BF16),
            vmem((heads, length, LANES), BF16),
            vmem((heads, length, LANES), BF16),
            vmem((heads, length, LANES), BF16),
            vmem((length, width), BF16),
            vmem((length, width), F32),
            vmem((length, units), BF16),
            vmem((length, units), BF16),
            vmem((width // LANES, length + 8, LANES), F32),
            vmem((short, 3 * width), BF16),
            vmem((length, width), BF16),
            vmem((short, width), BF16),
            vmem((short, width), BF16),
            vmem((short, width), BF16),
            vmem((length, width), BF16),
            pltpu.SemaphoreType.DMA((5,)),
            pltpu.SemaphoreType.DMA((4,)),
            pltpu.SemaphoreType.DMA((4,)),
            pltpu.SemaphoreType.DMA((5,)),
            pltpu.SemaphoreType.DMA((5,)),
            pltpu.SemaphoreType.DMA((3,)),
            pltpu.SemaphoreType.DMA((3,)),
            pltpu.SemaphoreType.DMA((24,)),
            pltpu.SemaphoreType.DMA((1,)),
            pltpu.SemaphoreType.DMA((1,)),
        ],
        compiler_params=pltpu.CompilerParams(
            collective_id=0, has_side_effects=True, vmem_limit_bytes=VMEM_LIMIT
        ),
        name="first",
    )(activations, cotangent, ids, gains, slopes, proj, out_rows, up_rows, down_rows)


def short_kernel(
    hidden_ref,
    grad_ref,
    gain_ref,
    query_mark_ref,
    key_mark_ref,
    proj_src,
    out_src,
    up_src,
    down_src,
    result_dst,
    hidden_dst,
    even_dst,
    out_dst,
    up_dst,
    down_dst,
    small_ref,
    proj_ref,
    out_ref,
    up_ref,
    down_ref,
    result_ref,
    hidden_grad,
    even_grad,
    out_grad,
    up_grad,
    down_grad,
    mixed,
    queries,
    keys,
    values,
    grads,
    key_sum,
    value_sum,
    attended,
    middle,
    total,
    normal,
    flip,
    grad_flip,
    actives,
    slants,
    attended_grad,
    mixed_grad,
    load_sem,
    done_sem,
    *,
    heads,
):
    length, width = hidden_ref.shape
    units = up_ref.shape[1]
    piece = units // PARTS
    loads = [
        pltpu.make_async_copy(origin, target, load_sem.at[index])
        for index, (origin, target) in enumerate(
            (
                (proj_src.at[0:width, :], proj_ref),
                (out_src, out_ref),
                (up_src, up_ref),
                (down_src, down_ref),
            )
        )
    ]
    for copy in loads:
        copy.start()
    lane = lane_ids(length)
    upper = lane >= HALF
    mark = lane % HALF
    earlier = lax.broadcasted_iota(jnp.int32, (length, length), 0) >= lax.broadcasted_iota(
        jnp.int32, (length, length), 1
    )
    standard, _ = standardize(hidden_ref[...].astype(F32))
    low = (standard * gain_ref[0:1, :]).astype(BF16)
    flip[...] = low.T
    loads[0].wait()
    mixed[...] = dot(low, proj_ref[...], 1, 0).astype(BF16)
    small_ref[...] = jnp.zeros_like(small_ref)
    column = lax.broadcasted_iota(jnp.int32, (1, width), 1)
    sides = (jnp.logical_not(upper), upper)
    per = heads // 2

    def attend_pair(pair, carry):
        cuts = head_cuts(pair, width)
        query_rows = mixed[:, cuts[0]].astype(F32) * 0.125
        key_rows = mixed[:, cuts[1]].astype(F32)
        value_rows = mixed[:, cuts[2]].astype(F32)
        scores, parts = [], []
        for side, here in enumerate(sides):
            number = 2 * pair + side
            slopes = jnp.where(number < per, gain_ref[1:2, :], gain_ref[9:10, :])
            slope = jnp.sum(jnp.where(column == number % per, slopes, 0.0), axis=1, keepdims=True)
            keys[side] = jnp.where(here, key_rows, key_mark_ref[...].astype(F32)).astype(BF16)
            values[side] = jnp.where(here, value_rows, 1.0).astype(BF16)
            marks = jnp.where(mark < 2, slope, query_mark_ref[...].astype(F32))
            query = jnp.where(here, query_rows, marks).astype(BF16)
            parts.append(query)
            scores.append(jnp.where(earlier, dot(query, keys[side], 1, 1), APART))
        shares = []
        for side, here in enumerate(sides):
            highest = jnp.max(scores[side], axis=1, keepdims=True)
            mass = dot(jnp.exp(scores[side] - highest).astype(BF16), values[side], 1, 0)
            level = -(highest + jnp.log(mass))
            first = level.astype(BF16).astype(F32)
            second = (level - first).astype(BF16).astype(F32)
            third = level - first - second
            query = parts[side].astype(F32)
            level_marks = jnp.where(
                mark == 5, first, jnp.where(mark == 6, second, jnp.where(mark == 7, third, query))
            )
            queries[2 * pair + side] = jnp.where(here, query, level_marks).astype(BF16)
            shares.append(mass / pltpu.roll(mass, HALF, 1))
        attended[:, cuts[0]] = jnp.where(upper, shares[1], shares[0]).astype(BF16)
        return carry

    lax.fori_loop(0, heads // 2, attend_pair, 0)
    loads[1].wait()
    value = hidden_ref[...].astype(F32) + dot(attended[...], out_ref[...], 1, 0)
    middle[...] = value
    total[...] = value
    standard, _ = standardize(value)
    normal[...] = (standard * gain_ref[8:9, :]).astype(BF16)
    loads[2].wait()
    loads[3].wait()
    for part in range(PARTS):
        span = slice(part * piece, (part + 1) * piece)
        raised = dot(normal[...], up_ref[:, span], 1, 0)
        active, slant = gelu_pieces(raised)
        active = active.astype(BF16)
        actives[:, span] = active
        slants[:, span] = slant.astype(BF16)
        total[...] += dot(active, down_ref[span, :], 1, 0)
    result_ref[...] = total[...].astype(BF16)
    results = [pltpu.make_async_copy(result_ref, result_dst, done_sem.at[0])]
    results[0].start()

    grad_flip[...] = grad_ref[...].T
    normal_flip = normal[...].T
    for part in range(PARTS):
        span = slice(part * piece, (part + 1) * piece)
        down_grad[span, :] = dot(grad_flip[...], actives[:, span], 1, 0).astype(BF16).T
        grad_active = dot(grad_ref[...], down_ref[span, :], 1, 1)
        low = (grad_active * slants[:, span].astype(F32)).astype(BF16)
        term = dot(low, up_ref[:, span], 1, 1)
        if part:
            total[...] += term
        else:
            total[...] = term
        up_grad[:, span] = dot(normal_flip, low, 1, 0).astype(BF16)
    for index, (origin, target) in enumerate(((down_grad, down_dst), (up_grad, up_dst))):
        results.append(pltpu.make_async_copy(origin, target, done_sem.at[1 + index]))
        results[-1].start()
    standard, inverse = standardize(middle[...])
    grad = total[...]
    small_ref[1:2, :] = jnp.sum(grad * standard, axis=0, keepdims=True)
    middle_grad = grad_ref[...].astype(F32) + norm_back(grad, gain_ref[8:9, :], standard, inverse)
    total[...] = middle_grad
    low = middle_grad.astype(BF16)
    attended_grad[...] = dot(low, out_ref[...], 1, 1).astype(BF16)
    out_grad[...] = dot(attended[...], low, 0, 0).astype(BF16)
    results.append(pltpu.make_async_copy(out_grad, out_dst, done_sem.at[3]))
    results[-1].start()

    def back_pair(pair, carry):
        cuts = head_cuts(pair, width)
        for side in range(2):
            slope_grad = head_back(
                side, key_mark_ref, queries.at[pl.ds(2 * pair + side, 1)], mixed.at[:, cuts[1]],
                mixed.at[:, cuts[2]], attended.at[:, cuts[0]], attended_grad.at[:, cuts[0]],
                mixed_grad, keys.at[side], values.at[side], grads.at[side], key_sum.at[side],
                value_sum.at[side], cuts, length,
            )
            small_ref[2:3, :] += jnp.where(column == 2 * pair + side, slope_grad, 0.0)
        return carry

    lax.fori_loop(0, heads // 2, back_pair, 0)
    for place in range(3):
        span = slice(place * width, (place + 1) * width)
        even_grad[:, span] = dot(flip[...], mixed_grad[:, span], 1, 0).astype(BF16)
    results.append(pltpu.make_async_copy(even_grad, even_dst, done_sem.at[4]))
    results[-1].start()
    standard, inverse = standardize(hidden_ref[...].astype(F32))
    grad = dot(mixed_grad[...], proj_ref[...], 1, 1)
    small_ref[0:1, :] = jnp.sum(grad * standard, axis=0, keepdims=True)
    hidden_grad[...] = (
        total[...] + norm_back(grad, gain_ref[0:1, :], standard, inverse)
    ).astype(BF16)
    results.append(pltpu.make_async_copy(hidden_grad, hidden_dst, done_sem.at[5]))
    results[-1].start()
    for copy in results:
        copy.wait()


def short_call(
    hidden, grad, gains, query_mark, key_mark, proj, out_weight, up_weight, down_weight, heads
):
    inside = pl.BlockSpec(memory_space=pltpu.VMEM)
    anywhere = pl.BlockSpec(memory_space=pl.ANY)
    length, width = hidden.shape
    units = up_weight.shape[1]
    vmem = pltpu.VMEM
    shape = jax.ShapeDtypeStruct
    grads = [(width, 3 * width), out_weight.shape, up_weight.shape, down_weight.shape]
    return pl.pallas_call(
        functools.partial(short_kernel, heads=heads),
        in_specs=[inside] * 5 + [anywhere] * 4,
        out_specs=[anywhere] * 6 + [inside],
        out_shape=[shape((length, width), BF16)] * 2
        + [shape(size, BF16) for size in grads]
        + [shape((8, width), F32)],
        scratch_shapes=[
            vmem((width, 3 * width), BF16),
            vmem(out_weight.shape, BF16),
            vmem(up_weight.shape, BF16),
            vmem(down_weight.shape, BF16),
            vmem((length, width), BF16),
            vmem((length, width), BF16),
        ]
        + [vmem(size, BF16) for size in grads]
        + [
            vmem((length, 3 * width), BF16),
            vmem((heads, length, LANES), BF16),
            vmem((2, length, LANES), BF16),
            vmem((2, length, LANES), BF16),
            vmem((2, length, LANES), BF16),
            vmem((2, length, LANES), F32),
            vmem((2, length, LANES), F32),
            vmem((length, width), BF16),
            vmem((length, width), F32),
            vmem((length, width), F32),
            vmem((length, width), BF16),
            vmem((width, length), BF16),
            vmem((width, length), BF16),
            vmem((length, units), BF16),
            vmem((length, units), BF16),
            vmem((length, width), BF16),
            vmem((length, 3 * width), BF16),
            pltpu.SemaphoreType.DMA((4,)),
            pltpu.SemaphoreType.DMA((6,)),
        ],
        compiler_params=params(),
        name="short",
    )(hidden, grad, gains, query_mark, key_mark, proj, out_weight, up_weight, down_weight)


def chunk_list():
    chunks = [("odd", 1, 0, 512, place * 512, 512) for place in range(3)]
    chunks += [("up", None, 0, 256, place * 512, 512) for place in (0, 2)]
    chunks += [("down", None, 0, 512, 0, 512)]
    chunks += [("up", None, 0, 256, place * 512, 512) for place in (1, 3)]
    chunks += [("down", None, 512, 512, 0, 512)]
    chunks += [("out", None, 0, 256, 0, 512)]
    chunks += [("even", 0, 0, 512, pair * 384, 384) for pair in range(4)]
    return chunks


BEGINS = {1: (3,), 2: (4, 5), 3: (6,), 4: (7, 8, 9), 6: (10,), 8: (11,), 10: (12,), 12: (13,)}
TICKS = {
    3: [
        ("pair", 3), ("side", 1), ("side", 2), ("line", 0),
    ],
    4: [
        ("pair", 5), ("side", 3), ("line", 1), ("line", 2), ("side", 4),
    ],
    5: [
        ("line", 3), ("side", 5),
    ],
    6: [
        ("back", 1), ("side", 6), ("pair", 7), ("pair", 9), ("back", 2), ("pair", 8),
        ("full", 0), ("line", 4),
    ],
    7: [
        ("full", 1), ("back", 3), ("side", 7),
    ],
    8: [
        ("pair", 10), ("side", 9), ("line", 5), ("full", 2), ("line", 6),
    ],
    9: [
        ("back", 4), ("side", 8),
    ],
    10: [
        ("line", 7), ("pair", 11), ("full", 3), ("line", 9), ("side", 10),
    ],
    11: [
        ("full", 4), ("back", 5), ("side", 11),
    ],
    12: [
        ("back", 6), ("pair", 12),
    ],
    13: [
        ("line", 8), ("full", 5),
    ],
}
MIDDLES = {
    1: [
        ("pair", 0), ("pair", 1), ("pair", 2),
    ],
    2: [
        ("side", 0),
    ],
    3: [
        ("pair", 4),
    ],
    4: [
        ("pair", 6), ("back", 0),
    ],
}
DRAIN = [
    ("full", 6), ("back", 7), ("pair", 13), ("side", 12), ("back", 9), ("line", 10),
    ("line", 11), ("full", 7), ("side", 13), ("back", 8), ("full", 9), ("line", 12),
    ("back", 10), ("back", 11), ("full", 8), ("line", 13), ("full", 10), ("back", 12),
    ("full", 11), ("back", 13), ("full", 12), ("full", 13),
]


def last_kernel(
    hidden_src,
    gain_ref,
    proj_src,
    key_mark_src,
    middle_src,
    attended_src,
    out_weight_src,
    keep_src,
    grouped_src,
    added_src,
    active_ref,
    slant_ref,
    up_weight_ref,
    down_weight_ref,
    query_ref,
    key_ref,
    value_ref,
    long_src,
    pooled_grad_ref,
    short_result_ref,
    even_ref,
    out_ref,
    up_ref,
    down_ref,
    small_ref,
    proj_result,
    out_result,
    up_result,
    down_result,
    small_result,
    parts_result,
    middle_ref,
    attended_ref,
    out_weight_ref,
    hidden_ref,
    key_mark_ref,
    proj_ref,
    keep_ref,
    grouped_ref,
    added_ref,
    sent_long,
    short_rows,
    sent_rows,
    moved,
    rows_buf,
    normal,
    grad_flip,
    total,
    lower,
    attended_grad,
    mixed,
    keys,
    values,
    grads,
    key_sum,
    value_sum,
    even_grad,
    odd_grad,
    out_grad,
    up_grad,
    down_grad,
    small_grad,
    small_full,
    parts_ref,
    proj_full,
    out_full,
    up_full,
    down_full,
    proj_pair,
    out_pair,
    up_pair,
    down_pair,
    proj_side,
    out_side,
    up_side,
    down_side,
    proj_line,
    out_line,
    up_line,
    down_line,
    small_pair,
    small_side,
    small_line,
    local_sem,
    pair_send,
    pair_recv,
    side_send,
    side_recv,
    line_send,
    line_recv,
    back_send,
    back_recv,
    full_send,
    full_recv,
    small_send,
    small_recv,
    rows_send,
    rows_recv,
    result_sem,
    load_sem,
    short_send,
    short_recv,
    early_sem,
    *,
    tile,
):
    step = pl.program_id(0)
    last = pl.num_programs(0) - 1
    section = lax.axis_index("section")
    group = lax.axis_index("dp")
    core = section % 2
    chip = section // 2
    partner = (chip * 2 + (1 - core), group)
    base = group // SQUARE * SQUARE
    side = group % 2
    line = group % SQUARE // 2
    neighbour = (section, base + line * 2 + (1 - side))
    length, width = hidden_ref.shape
    short = length // 3
    groups = width // LANES
    stride = min(length // 2, 384)
    quarter = parts_ref.shape[1]
    chunks = chunk_list()
    first_head = 1 + PARTS

    def along(hop):
        return (section, base + lax.rem(line + hop, LINE) * 2 + side)

    def across(hop):
        return lax.rem(section + hop, 4)

    source = {"odd": odd_grad, "even": even_grad, "out": out_grad, "up": up_grad, "down": down_grad}
    table = lambda proj, out, up, down: {
        "odd": proj, "even": proj, "out": out, "up": up, "down": down
    }
    sums = table(proj_pair, out_pair, up_pair, down_pair)
    sides = table(proj_side, out_side, up_side, down_side)
    lines = table(proj_line, out_line, up_line, down_line)
    fulls = table(proj_full, out_full, up_full, down_full)
    outcomes = table(proj_result, out_result, up_result, down_result)

    def cut(start, size):
        return pl.ds(pl.multiple_of(start, 16), size)

    def remote(origin, target, send, recv, device):
        return pltpu.make_async_remote_copy(
            src_ref=origin,
            dst_ref=target,
            send_sem=send,
            recv_sem=recv,
            device_id=device,
            device_id_type=MESH,
        )

    def pair_copy(index):
        name, owner, start, rows, left, cols = chunks[index]
        offset = 0 if owner is not None else (1 - core) * (source[name].shape[0] // 2)
        lanes = pl.ds(left, cols)
        return remote(
            source[name].at[cut(offset + start, rows), lanes],
            sums[name].at[cut(start, rows), lanes],
            pair_send.at[index],
            pair_recv.at[index],
            partner,
        )

    def side_copy(index):
        name, _, start, rows, left, cols = chunks[index]
        half = rows // 2
        lanes = pl.ds(left, cols)
        return remote(
            sums[name].at[cut(start + (1 - side) * half, half), lanes],
            sides[name].at[cut(start // 2, half), lanes],
            side_send.at[index],
            side_recv.at[index],
            neighbour,
        )

    def line_copy(index, hop):
        name, _, start, rows, left, cols = chunks[index]
        half, piece = rows // 2, rows // SQUARE
        lanes = pl.ds(left, cols)
        target = lax.rem(line + hop, LINE)
        return remote(
            sums[name].at[cut(start + side * half + target * piece, piece), lanes],
            lines[name].at[hop - 1, cut(start // SQUARE, piece), lanes],
            line_send.at[index, hop - 1],
            line_recv.at[index, hop - 1],
            along(hop),
        )

    def back_copy(index, hop):
        name, _, start, rows, left, cols = chunks[index]
        half, piece = rows // 2, rows // SQUARE
        place = fulls[name].at[
            cut(start + side * half + line * piece, piece), pl.ds(left, cols)
        ]
        return remote(
            place, place, back_send.at[index, hop - 1], back_recv.at[index, hop - 1], along(hop)
        )

    def full_copy(index):
        name, _, start, rows, left, cols = chunks[index]
        half = rows // 2
        place = fulls[name].at[cut(start + side * half, half), pl.ds(left, cols)]
        return remote(place, place, full_send.at[index], full_recv.at[index], neighbour)

    def result_copies(index):
        name, _, start, rows, left, cols = chunks[index]
        spans = [(pl.ds(left, cols), pl.ds(left, cols))]
        if name == "even":
            spans = [span for span in regroup() if left <= span[1].start < left + cols]
        return [
            pltpu.make_async_copy(
                fulls[name].at[cut(start, rows), held],
                outcomes[name].at[cut(start, rows), final],
                result_sem.at[index, number],
            )
            for number, (final, held) in enumerate(spans)
        ]

    def owned(index, act):
        owner = chunks[index][1]
        if owner is None:
            act()
        else:
            pl.when(core == owner)(act)

    def pair_start(index):
        owner = chunks[index][1]
        begin = lambda: pair_copy(index).start()
        if owner is None:
            begin()
        else:
            pl.when(core != owner)(begin)

    def pair_stage(index):
        name, owner, start, rows, left, cols = chunks[index]
        lanes = slice(left, left + cols)
        here = cut(start, rows)

        def act():
            pair_copy(index).wait_recv()
            offset = 0 if owner is not None else core * (source[name].shape[0] // 2)
            mine = source[name][cut(offset + start, rows), lanes].astype(F32)
            arrived = sums[name][here, lanes].astype(F32)
            sums[name][here, lanes] = (mine + arrived).astype(BF16)
            side_copy(index).start()

        if owner is None:
            pair_copy(index).wait_send()
        else:
            pl.when(core != owner)(lambda: pair_copy(index).wait_send())
        owned(index, act)

    def side_stage(index):
        name, _, start, rows, left, cols = chunks[index]
        half = rows // 2
        lanes = slice(left, left + cols)

        def act():
            side_copy(index).wait()
            here = cut(start + side * half, half)
            arrived = sides[name][cut(start // 2, half), lanes].astype(F32)
            sums[name][here, lanes] = (sums[name][here, lanes].astype(F32) + arrived).astype(BF16)
            for hop in range(1, LINE):
                line_copy(index, hop).start()

        owned(index, act)

    def line_stage(index):
        name, _, start, rows, left, cols = chunks[index]
        half, piece = rows // 2, rows // SQUARE
        lanes = slice(left, left + cols)

        def act():
            for hop in range(1, LINE):
                line_copy(index, hop).wait()
            here = cut(start + side * half + line * piece, piece)
            value = sums[name][here, lanes].astype(F32)
            for hop in range(1, LINE):
                value = value + lines[name][hop - 1, cut(start // SQUARE, piece), lanes].astype(F32)
            fulls[name][here, lanes] = value.astype(BF16)
            for hop in range(1, LINE):
                back_copy(index, hop).start()

        owned(index, act)

    def back_stage(index):
        def act():
            for hop in range(1, LINE):
                back_copy(index, hop).wait()
            full_copy(index).start()

        owned(index, act)

    def full_stage(index):
        def act():
            full_copy(index).wait()
            for copy in result_copies(index):
                copy.start()

        owned(index, act)

    def result_wait(index):
        for copy in result_copies(index):
            copy.wait()

    stages = {
        "pair": pair_stage,
        "side": side_stage,
        "line": line_stage,
        "back": back_stage,
        "full": full_stage,
    }

    def rows_copy(hop):
        target = across(hop)
        return remote(
            rows_buf.at[cut(target * quarter, quarter), :],
            parts_ref.at[section],
            rows_send.at[hop],
            rows_recv.at[hop],
            (target, group),
        )

    def load_copies():
        pairs = [
            (out_ref, out_grad),
            (up_ref, up_grad),
            (down_ref, down_grad),
            (small_ref, small_grad),
        ]
        pairs += [
            (even_ref.at[:, origin], even_grad.at[:, target]) for origin, target in regroup()
        ]
        return [
            pltpu.make_async_copy(origin, target, load_sem.at[index])
            for index, (origin, target) in enumerate(pairs)
        ]

    def regroup():
        for pair in range(width // LANES):
            for place in range(3):
                yield (
                    pl.ds(place * width + pair * LANES, LANES),
                    pl.ds((3 * pair + place) * LANES, LANES),
                )

    def kept_copies(members=range(5)):
        pairs = (
            (middle_src, middle_ref),
            (attended_src, attended_ref),
            (out_weight_src, out_weight_ref),
            (hidden_src, hidden_ref),
            (key_mark_src, key_mark_ref),
        )
        return [
            pltpu.make_async_copy(*pairs[member], local_sem.at[1 + member]) for member in members
        ]

    def early_copies(members):
        pairs = (
            (grouped_src, grouped_ref),
            (proj_src, proj_ref),
            (keep_src, keep_ref),
            (added_src, added_ref),
            (long_src, sent_long),
        )
        return [
            pltpu.make_async_copy(*pairs[member], early_sem.at[member]) for member in members
        ]

    def early_wait(*members):
        for copy in early_copies(members):
            copy.wait()

    def long_copy():
        return remote(
            sent_long, added_ref, short_send.at[1], short_recv.at[1], (across(2), group)
        )

    def kept_wait(*members):
        for copy in kept_copies(members):
            copy.wait()

    @pl.when(step == 0)
    def _():
        @pl.when(chip == 0)
        def _():
            for copy in early_copies(range(5)):
                copy.start()
            for copy in kept_copies():
                copy.start()
            small_grad[...] = jnp.zeros_like(small_grad)

        @pl.when(chip == 1)
        def _():
            pltpu.make_async_copy(pooled_grad_ref, sent_rows, local_sem.at[0]).start()
            pltpu.make_async_copy(short_result_ref, short_rows, local_sem.at[6]).start()
            for copy in early_copies(range(3)):
                copy.start()
            for copy in load_copies():
                copy.start()

        barrier_with(
            [(across(hop), group) for hop in range(1, 4)]
            + [neighbour]
            + [along(hop) for hop in range(1, LINE)]
        )
        short_copy = remote(
            sent_rows, short_rows, short_send.at[0], short_recv.at[0], (across(2), group)
        )

        @pl.when(chip == 0)
        def _():
            early_wait(4)
            long_copy().start()
            kept_wait(0)
            for rows in row_cuts(length, stride):
                standard, _ = standardize(middle_ref[rows, :])
                normal[:, rows] = (standard * gain_ref[8:9, :]).astype(BF16).T
                total[rows, :] = jnp.zeros((stride, width), F32)
            early_wait(3)
            short_copy.wait_recv()

        @pl.when(chip == 1)
        def _():
            pltpu.make_async_copy(pooled_grad_ref, sent_rows, local_sem.at[0]).wait()
            short_copy.start()
            pltpu.make_async_copy(short_result_ref, short_rows, local_sem.at[6]).wait()

        early_wait(0, 1, 2)
        rows = short_rows[...]
        flip = rows.T
        for place in range(3):
            lanes = slice(place * width, (place + 1) * width)
            odd_grad[:, lanes] = dot(flip, grouped_ref[:, lanes], 1, 0).astype(BF16)
            pair_start(place)
        for place in range(3):
            lanes = slice(place * width, (place + 1) * width)
            spread_rows = dot(rows, proj_ref[width : 2 * width, lanes], 1, 0)
            factor = jnp.maximum(keep_ref[place], chip.astype(F32))
            for part in range(groups):
                moved[part, pl.ds(place, short, stride=3), :] = (
                    spread_rows[:, part * LANES : (part + 1) * LANES] * factor
                )
        for part in range(groups):
            moved[part, length:, :] = jnp.zeros((8, LANES), F32)

        @pl.when(chip == 0)
        def _():
            for part in range(groups):
                lanes = slice(part * LANES, (part + 1) * LANES)
                rows_buf[:, lanes] = (
                    added_ref[:, lanes].astype(F32) + moved[part, 2 : 2 + length, :]
                ).astype(BF16)

        @pl.when(chip == 1)
        def _():
            for copy in load_copies():
                copy.wait()
            short_copy.wait_send()

    for tick, events in TICKS.items():

        @pl.when(step == tick)
        def _():
            for stage, index in events:
                stages[stage](index)

    @pl.when((chip == 0) & (step == 1))
    def _():
        for rows in row_cuts(length, stride):
            grad_flip[:, rows] = rows_buf[rows, :].T

    @pl.when((chip == 0) & (step >= 1) & (step < first_head))
    def _():
        turn = step - 1
        part = (turn % 2) * 2 + turn // 2
        span = pl.ds(pl.multiple_of(part * 512, 512), 512)
        down_grad[span, :] = dot(grad_flip[...], active_ref[...], 1, 0).astype(BF16).T

    for tick, events in MIDDLES.items():

        @pl.when(step == tick)
        def _():
            for stage, index in events:
                stages[stage](index)

    @pl.when((chip == 0) & (step >= 1) & (step < first_head))
    def _():
        turn = step - 1
        part = (turn % 2) * 2 + turn // 2
        span = pl.ds(pl.multiple_of(part * 512, 512), 512)
        for rows in row_cuts(length, stride):
            grad_active = dot(rows_buf[rows, :], down_weight_ref[...], 1, 1)
            low = (grad_active * slant_ref[rows, :].astype(F32)).astype(BF16)
            lower[rows, :] = low
            total[rows, :] += dot(low, up_weight_ref[...], 1, 1)
        up_grad[:, span] = dot(normal[...], lower[...], 1, 0).astype(BF16)

    @pl.when((chip == 0) & (step == first_head - 1))
    def _():
        kept_wait(1, 2)
        gain_sum = jnp.zeros((1, width), F32)
        for rows in row_cuts(length, stride):
            standard, inverse = standardize(middle_ref[rows, :])
            grad = total[rows, :]
            gain_sum = gain_sum + jnp.sum(grad * standard, axis=0, keepdims=True)
            middle_grad = rows_buf[rows, :].astype(F32) + norm_back(
                grad, gain_ref[8:9, :], standard, inverse
            )
            total[rows, :] = middle_grad
            low = middle_grad.astype(BF16)
            lower[rows, :] = low
            attended_grad[rows, :] = dot(low, out_weight_ref[...], 1, 1).astype(BF16)
        small_grad[1:2, :] = gain_sum
        out_grad[...] = dot(attended_ref[...], lower[...], 0, 0).astype(BF16)

    @pl.when((chip == 0) & (step == first_head))
    def _():
        kept_wait(3, 4)
        for rows in row_cuts(length, stride):
            standard, _ = standardize(hidden_ref[rows, :].astype(F32))
            normal[:, rows] = (standard * gain_ref[0:1, :]).astype(BF16).T

    @pl.when((chip == 0) & (step >= first_head) & (step < last))
    def _():
        head = step - first_head
        cuts = head_cuts(head // 2, width)
        slope_grad = head_back(
            head % 2, key_mark_ref, query_ref, key_ref, value_ref, attended_ref.at[:, cuts[0]],
            attended_grad.at[:, cuts[0]], mixed, keys, values, grads, key_sum, value_sum,
            cuts, tile,
        )
        column = lax.broadcasted_iota(jnp.int32, (1, width), 1)
        small_grad[2:3, :] += jnp.where(column == head, slope_grad, 0.0)

    @pl.when((chip == 0) & (step >= first_head) & (step < last) & (step % 2 == 0))
    def _():
        pair = (step - first_head) // 2
        for place, span in enumerate(head_cuts(pair, width)):
            target = pl.ds(pl.multiple_of((3 * pair + place) * LANES, LANES), LANES)
            even_grad[:, target] = dot(normal[...], mixed[:, span], 1, 0).astype(BF16)

    for begin, members in BEGINS.items():
        @pl.when(step == begin)
        def _():
            for index in members:
                pair_start(index)

    @pl.when((chip == 0) & (step == last))
    def _():
        gain_sum = jnp.zeros((1, width), F32)
        for rows in row_cuts(length, stride):
            standard, inverse = standardize(hidden_ref[rows, :].astype(F32))
            grad = dot(mixed[rows, :], proj_ref[0:width, :], 1, 1)
            gain_sum = gain_sum + jnp.sum(grad * standard, axis=0, keepdims=True)
            rows_buf[rows, :] = (
                total[rows, :] + norm_back(grad, gain_ref[0:1, :], standard, inverse)
            ).astype(BF16)
        small_grad[0:1, :] = gain_sum

    @pl.when((chip == 0) & (step == last))
    def _():
        long_copy().wait_send()

    @pl.when((chip == 1) & (step == last))
    def _():
        long_copy().wait_recv()
        for part in range(groups):
            lanes = slice(part * LANES, (part + 1) * LANES)
            rows_buf[:, lanes] = (
                added_ref[:, lanes].astype(F32) + moved[part, 0:length, :]
            ).astype(BF16)

    @pl.when(step == last)
    def _():
        small_one = remote(small_grad, small_pair, small_send.at[0], small_recv.at[0], partner)
        small_one.start()
        for hop in range(1, 4):
            rows_copy(hop).start()
        parts_ref[section] = rows_buf[cut(section * quarter, quarter), :]
        for stage, index in DRAIN[:3]:
            stages[stage](index)
        small_one.wait()
        small_full[...] = small_grad[...] + small_pair[...]
        small_two = remote(small_full, small_side, small_send.at[1], small_recv.at[1], neighbour)
        small_two.start()
        for stage, index in DRAIN[3:7]:
            stages[stage](index)
        small_two.wait()
        small_full[...] = small_full[...] + small_side[...]
        small_rest = [
            remote(
                small_full,
                small_line.at[line],
                small_send.at[1 + hop],
                small_recv.at[1 + hop],
                along(hop),
            )
            for hop in range(1, LINE)
        ]
        for copy in small_rest:
            copy.start()
        for stage, index in DRAIN[7:]:
            stages[stage](index)
        for copy in small_rest:
            copy.wait()
        small_line[line] = small_full[...]
        small_result[...] = (small_line[0] + small_line[1]) + (small_line[2] + small_line[3])
        for hop in range(1, 4):
            rows_copy(hop).wait()
        parts_copy = pltpu.make_async_copy(parts_ref, parts_result, result_sem.at[len(chunks), 0])
        parts_copy.start()
        for index in range(len(chunks)):
            owned(index, functools.partial(result_wait, index))
        parts_copy.wait()


def last_call(
    hidden, gains, proj, key_mark, middle, attended, out_weight, keep, grouped, added,
    active, slant, up_weight, down_weight, query, keyval,
    long_rows, pooled_grad, short_result, even, out_grad, up_grad, down_grad, small, tile,
):
    inside = pl.BlockSpec(memory_space=pltpu.VMEM)
    anywhere = pl.BlockSpec(memory_space=pl.ANY)
    length, width = hidden.shape
    short = length // 3
    heads = query.shape[0]
    units = up_weight.shape[1]
    wide = even.shape[1]
    piece = units // PARTS
    half = lambda value: (value.shape[0] // 2, value.shape[1])
    shapes = [even.shape, half(out_grad), half(up_grad), half(down_grad)]
    count = len(chunk_list())
    vmem = pltpu.VMEM
    scaled = lambda over: [vmem((rows // over, cols), BF16) for rows, cols in shapes]
    semaphores = lambda *shape: [pltpu.SemaphoreType.DMA(shape)] * 2

    def part_of(step):
        turn = jnp.clip(step - 1, 0, PARTS - 1)
        return turn % 2 * 2 + turn // 2

    def head_of(step):
        return jnp.clip(step - 1 - PARTS, 0, heads - 1)

    column = lambda start: pl.BlockSpec(
        (length, LANES), lambda step: (0, start + head_of(step) // 2)
    )
    results = pl.pallas_call(
        functools.partial(last_kernel, tile=tile),
        grid=(2 + PARTS + heads,),
        in_specs=[anywhere, inside] + [anywhere] * 8
        + [pl.BlockSpec((length, piece), lambda step: (0, part_of(step)))] * 2
        + [
            pl.BlockSpec((width, piece), lambda step: (0, part_of(step))),
            pl.BlockSpec((piece, width), lambda step: (part_of(step), 0)),
            pl.BlockSpec((1, length, LANES), lambda step: (head_of(step), 0, 0)),
            column(0),
            column(heads // 2),
        ]
        + [anywhere] * 8,
        out_specs=[anywhere] * 4 + [inside, anywhere],
        out_shape=[jax.ShapeDtypeStruct(shape, BF16) for shape in shapes]
        + [
            jax.ShapeDtypeStruct(small.shape, F32),
            jax.ShapeDtypeStruct((4, length // 4, width), BF16),
        ],
        scratch_shapes=[
            vmem((length, width), F32),
            vmem((length, width), BF16),
            vmem((width, width), BF16),
            vmem((length, width), BF16),
            vmem((length, LANES), BF16),
            vmem(proj.shape, BF16),
            vmem(keep.shape, F32),
            vmem(grouped.shape, BF16),
            vmem((length, width), BF16),
            vmem((length, width), BF16),
            vmem((short, width), BF16),
            vmem((short, width), BF16),
            vmem((width // LANES, length + 8, LANES), F32),
            vmem((length, width), BF16),
            vmem((width, length), BF16),
            vmem((width, length), BF16),
            vmem((length, width), F32),
            vmem((length, width), BF16),
            vmem((length, width), BF16),
            vmem((length, 3 * width), BF16),
            vmem((length, LANES), BF16),
            vmem((length, LANES), BF16),
            vmem((length, LANES), BF16),
            vmem((length, LANES), F32),
            vmem((length, LANES), F32),
            vmem((width, wide), BF16),
            vmem((width, wide), BF16),
            vmem(out_grad.shape, BF16),
            vmem(up_grad.shape, BF16),
            vmem(down_grad.shape, BF16),
            vmem(small.shape, F32),
            vmem(small.shape, F32),
            vmem((4, length // 4, width), BF16),
        ]
        + scaled(1)
        + scaled(1)
        + scaled(2)
        + [vmem((LINE - 1, rows // SQUARE, cols), BF16) for rows, cols in shapes]
        + [vmem(small.shape, F32)] * 2
        + [vmem((LINE,) + small.shape, F32)]
        + [pltpu.SemaphoreType.DMA((7,))]
        + semaphores(count)
        + semaphores(count)
        + semaphores(count, LINE - 1)
        + semaphores(count, LINE - 1)
        + semaphores(count)
        + semaphores(2 + LINE - 1)
        + semaphores(4)
        + [pltpu.SemaphoreType.DMA((count + 1, 3)), pltpu.SemaphoreType.DMA((16,))]
        + semaphores(2)
        + [pltpu.SemaphoreType.DMA((5,))],
        compiler_params=pltpu.CompilerParams(
            collective_id=1, has_side_effects=True, vmem_limit_bytes=VMEM_LIMIT
        ),
        name="last",
    )(
        hidden, gains, proj, key_mark, middle, attended, out_weight, keep, grouped, added,
        active, slant, up_weight, down_weight, query, keyval, keyval, long_rows,
        pooled_grad, short_result, even, out_grad, up_grad, down_grad, small,
    )
    parts = results[-1]
    results = results[:-1]
    squares = lax.axis_size("dp") // SQUARE
    if squares > 1:
        members = [
            [number * SQUARE + place for number in range(squares)] for place in range(SQUARE)
        ]
        results = lax.psum(results, "dp", axis_index_groups=members)
    return results, parts


def widen_kernel(*refs):
    step = pl.program_id(0)
    half = pl.num_programs(0) // 2
    core = lax.axis_index("section") % 2
    inputs = len(refs) // 2 - 1
    *sources, parts_ref, small_ref = refs[:inputs]
    *targets, input_ref, results_ref, gain_ref, slope_ref = refs[inputs:]
    mine = jnp.where(core == 0, small_ref[0:1, :], small_ref[1:2, :])
    gain_ref[...] = mine
    per = slope_ref.shape[1]
    slope_ref[...] = jnp.where(core == 0, small_ref[2:3, 0:per], small_ref[2:3, per : 2 * per])
    for source, target in zip(sources, targets):
        target[...] = source[...].astype(F32)

    @pl.when(step < half)
    def _():
        input_ref[...] = parts_ref[...].astype(F32)

    @pl.when(step >= half)
    def _():
        results_ref[...] = parts_ref[...]


def widen_call(grads, parts, small, per):
    width = small.shape[1]
    whole = lambda *shape: pl.BlockSpec(shape, lambda step: (0, 0))
    steps = parts.shape[0]
    half = steps // 2
    block = lambda value: pl.BlockSpec(
        (value.shape[0] // steps, value.shape[1]), lambda step: (step, 0)
    )
    page = (1,) + parts.shape[1:]
    return pl.pallas_call(
        widen_kernel,
        grid=(steps,),
        in_specs=[block(value) for value in grads]
        + [pl.BlockSpec(page, lambda step: (step, 0, 0)), whole(*small.shape)],
        out_specs=[block(value) for value in grads]
        + [
            pl.BlockSpec(page, lambda step: (jnp.minimum(step, half - 1), 0, 0)),
            pl.BlockSpec(page, lambda step: (jnp.maximum(step - half, 0), 0, 0)),
            whole(1, width),
            whole(1, per),
        ],
        out_shape=[jax.ShapeDtypeStruct(value.shape, F32) for value in grads]
        + [
            jax.ShapeDtypeStruct((half,) + parts.shape[1:], F32),
            jax.ShapeDtypeStruct((half,) + parts.shape[1:], BF16),
            jax.ShapeDtypeStruct((1, width), F32),
            jax.ShapeDtypeStruct((1, per), F32),
        ],
        compiler_params=params(),
        name="widen",
    )(*grads, parts, small)


def body(
    activations,
    cotangent,
    article_ids,
    section_proj,
    out_rows,
    up_rows,
    down_rows,
    norm_gains,
    slopes,
):
    section = lax.axis_index("section")
    first_chip = section < 2
    width = activations.shape[3]
    length = article_ids.shape[2]
    short = length // 3
    heads = 2 * slopes.shape[1]
    tile = length // 3

    (
        row, proj, out_weight, up_weight, down_weight, query, keyval, attended, middle, active,
        slant, grouped, long_rows, pooled, short_grad, added, gains, key_mark, short_query_mark,
        short_key_mark, keep,
    ) = first_call(
        activations, cotangent, article_ids, norm_gains, slopes, section_proj[0], out_rows,
        up_rows, down_rows, heads, tile,
    )

    def zeros_of(call, *operands):
        return jax.tree.map(
            lambda leaf: jnp.zeros(leaf.shape, leaf.dtype), jax.eval_shape(call, *operands)
        )

    def short_all(pooled, grad):
        return short_call(
            pooled, grad, gains, short_query_mark, short_key_mark, proj, out_weight, up_weight,
            down_weight, heads,
        )

    short_result, pooled_grad, *short_grads = lax.cond(
        first_chip,
        lambda *operands: zeros_of(short_all, *operands),
        short_all,
        pooled,
        short_grad,
    )
    (proj_grad, out_grad, up_grad, down_grad, small), parts = last_call(
        row, gains, proj, key_mark, middle, attended, out_weight, keep, grouped, added,
        active, slant, up_weight, down_weight, query, keyval,
        long_rows, pooled_grad, short_result, *short_grads, tile=tile,
    )
    proj_grad, out_grad, up_grad, down_grad, input_grad, results, gain_grad, slope_grad = (
        widen_call((proj_grad, out_grad, up_grad, down_grad), parts, small, heads // 2)
    )
    return (
        results[:, None],
        input_grad[:, None],
        proj_grad[None],
        out_grad,
        up_grad,
        down_grad,
        gain_grad,
        slope_grad,
    )


def solution(mesh):
    return jax.shard_map(
        body,
        mesh=mesh,
        in_specs=(
            P(None, "dp", "section", None),
            P(None, "dp", "section", None),
            P(None, "dp", None),
            P("section", None, None),
            P("section", None),
            P("section", None),
            P("section", None),
            P("section", None),
            P("section", None),
        ),
        out_specs=(
            P(None, "dp", "section", None),
            P(None, "dp", "section", None),
            P("section", None, None),
            P("section", None),
            P("section", None),
            P("section", None),
            P("section", None),
            P("section", None),
        ),
        check_vma=False,
    )
```
